512 devices in a mesh: seq: 64 (over y, z), batch: 8 (over x, core).
Axes of the slice: x: 4, y: 4, z: 16, core: 2. Of those that a mesh axis runs over, the one named last changes fastest.
Arguments:
- queries: bfloat16 [8, 8192, 2048], P('batch', 'seq'), may hold values from -6 to 6
- out_grad: bfloat16 [8, 8192, 2048], P('batch', 'seq'), may hold values from -6 to 6
- states: bfloat16 [8, 1024, 8, 896], P('batch', 'seq'), may hold values from -6 to 6
- gain: float32 [896], replicated, may hold values from 0.25 to 1.75
- kv_weight: bfloat16 [896, 2, 2048], P('batch'), may hold values from -0.1875 to 0.1875
- owners: int32 [8, 128, 8], P('batch', 'seq'), may hold values from 0 to 63, all different within a row; in each aligned block of 2 rows (0 to 1, 2 to 3, ..., all dimensions but the last counted through in order) at most 2 rows name the same one
- slots: int32 [8, 128, 8], P('batch', 'seq'), may hold values from 0 to 15
Outputs:
- query_grad: bfloat16 [8, 8192, 2048], P('batch', 'seq')
- state_grad: bfloat16 [8, 1024, 8, 896], P('batch', 'seq')
- gain_grad: float32 [896], replicated
The draws below stay inside these ranges and needn't reach their ends.
Inputs may be any that keep to these rules, and one draw needn't show every extreme that they name: `owners`: the 8 entries of a group differ; in each aligned block of 2 groups (the groups of one device) no shard is named more than 2 times, and some block names one exactly 2 times.
All inputs are finite; a program needn't handle non-finite values.
Results may differ from the reference program's by a relative error of at most 0.0089.
Values may be sent and summed in bfloat16 or wider, within the bound.
A program may use at most 128 MiB of HBM per device.

```python
import math
import jax
import jax.numpy as jnp
import numpy as np
from jax import lax

D_ENC = 896
HEADS = 16
HEAD_DIM = 128
GROUP = 64
NL = 8
NB_DEV = 16
RETR = 8
QW = 2048
CH_DEV = 2
CAP = 2
TOKENS = 8192
GROUPS = 128
NEIGHS = 1024
SEQS = 8
N_SEQ = 64


def touch_ends(result, key, least, largest):
    index_at = [jax.random.randint(jax.random.fold_in(key, axis), (), 0, length) for axis, length in enumerate(result.shape)]
    longest = result.shape.index(max(result.shape))
    next_to = index_at[:longest] + [(index_at[longest] + 1) % result.shape[longest]] + index_at[longest + 1:]
    return result.at[tuple(index_at)].set(least).at[tuple(next_to)].set(largest)


def block_scale(rng, shape, shards, smallest, largest):
    level, own = 1.0, jax.random.fold_in(rng, 6)
    for position, blocks in shards:
        draws = jnp.exp(jax.random.uniform(jax.random.fold_in(own, position), (blocks,), jnp.float32, smallest / len(shards), largest / len(shards)))
        level = level * jnp.repeat(draws, shape[position] // blocks).reshape([-1 if axis == position else 1 for axis in range(len(shape))])
    return level


def routed_block(own_key, own, number, rows, count, top, limit, slope):
    order = jax.random.permutation(own_key, count)
    heavy_load, common = portions_of(count, rows * top, limit, slope, True), portions_of(count, rows * top, limit, slope, False)
    places = jnp.arange(count)

    def named(lengths, rotation):
        used = int((lengths > 0).sum())
        fixed = max(1, used // 4)
        moved = fixed + (places - fixed + rotation * (used - fixed)) % max(1, count - fixed)
        return jnp.zeros((count,), jnp.int32).at[order[jnp.where(places < fixed, places, moved)]].set(jnp.asarray(lengths, jnp.int32))

    lengths = jnp.where(number % 4 == 0, named(heavy_load, number // 4), named(common, number - number // 4 - 1))
    mixed = jax.random.permutation(jax.random.fold_in(own, 3), count)
    source_of, receiver = mixed[0:count // 2 * 2:2], mixed[1:count // 2 * 2:2]
    room = jnp.minimum(lengths[source_of] - 1, limit - lengths[receiver]) // 2
    room = jnp.where((source_of == order[0]) | (receiver == order[0]) | (lengths[receiver] == 0), 0, jnp.maximum(room, 0))
    moved = jax.random.randint(jax.random.fold_in(own, 4), (count // 2,), 0, 1 << 20) % (room + 1)
    lengths = lengths.at[source_of].add(-moved).at[receiver].add(moved)
    items = jnp.searchsorted(jnp.cumsum(lengths), jnp.arange(rows * top), side="right").astype(jnp.int32)
    table = items.reshape(top, rows).T
    table = table[jax.random.permutation(jax.random.fold_in(own, 1), rows)]
    rotation = jax.random.randint(jax.random.fold_in(own, 2), (rows, 1), 0, top)
    return jnp.take_along_axis(table, (jnp.arange(top)[None, :] + rotation) % top, axis=1)


def portions_of(number_of, total, bound, slope, full):
    portions = [(1 << 20) // math.isqrt(grade ** slope) + 1 for grade in range(1, number_of + 1)]
    largest = bound if full else min(bound, max(-(-total // number_of), total * portions[0] // sum(portions)))
    least = 1 if total - largest >= number_of - 1 else 0
    given, rest = [largest] + [least] * (number_of - 1), total - largest - least * (number_of - 1)
    while rest > 0:
        candidates = [i for i in range(1, number_of) if given[i] < largest] or [i for i in range(1, number_of) if given[i] < bound]
        mass, budget = sum([portions[i] for i in candidates]), rest
        for i in candidates:
            extra = min(bound - given[i], max(1, budget * portions[i] // mass), rest)
            given[i] = given[i] + extra
            rest = rest - extra
    return np.array(given)


def gaussian(stream_key, shape, scale, bound, shards=(), kind=jnp.bfloat16):
    values = scale * jax.random.normal(stream_key, shape, jnp.float32)
    if shards:
        values = values * block_scale(stream_key, shape, shards, -0.22, 0.18)
    return jnp.clip(values, -bound, bound).astype(kind)


def setup_inputs(seed: int = 0) -> dict:
    key_of = jax.random.split(jax.random.key(seed), 8)
    queries = gaussian(key_of[0], (SEQS, TOKENS, QW), 1.0, 6.0, ((0, 8), (1, 64)))
    out_grad = gaussian(key_of[1], (SEQS, TOKENS, QW), 1.0, 6.0, ((0, 8), (1, 64)))
    states = gaussian(key_of[2], (SEQS, NEIGHS, NL, D_ENC), 1.0, 6.0, ((0, 8), (1, 64)))
    gain = jnp.clip(1.0 + 0.15 * jax.random.normal(key_of[3], (D_ENC,), jnp.float32), 0.25, 1.75)
    kv_weight = gaussian(key_of[4], (D_ENC, 2, QW), D_ENC ** -0.5, 0.1875, ((0, 8),))
    owners_keys = jax.random.split(jax.random.fold_in(key_of[5], 1), SEQS * GROUPS // CH_DEV)
    owners_turns = jax.random.permutation(jax.random.fold_in(key_of[5], 3), SEQS * GROUPS // CH_DEV)
    owners = jax.vmap(lambda own, number: routed_block(jax.random.fold_in(key_of[5], 2), own, number, CH_DEV, N_SEQ, RETR, CAP, 2))(owners_keys, owners_turns).reshape((SEQS, GROUPS, RETR))
    slots = touch_ends(jax.random.randint(key_of[6], (SEQS, GROUPS, RETR), 0, NB_DEV), jax.random.fold_in(key_of[6], 1), 0, NB_DEV - 1).astype(jnp.int32)
    return {"queries": queries, "out_grad": out_grad, "states": states, "gain": gain, "kv_weight": kv_weight, "owners": owners, "slots": slots}


EPS = 1e-06

def block_backward(query_block, grad_block, key_block, value_block):
    scaling = 1.0 / math.sqrt(HEAD_DIM)
    query_wide = query_block.astype(jnp.float32)
    grad_wide = grad_block.astype(jnp.float32)
    key_wide = key_block.astype(jnp.float32)
    value_wide = value_block.astype(jnp.float32)
    scores = jnp.einsum('uqhe,ukhe->uhqk', query_wide, key_wide) * scaling
    weights = jnp.exp(scores)
    probability = weights / lax.optimization_barrier(jnp.sum(weights, axis=-1, keepdims=True))
    probability_low = probability.astype(jnp.bfloat16)
    grad_probability = jnp.einsum('uqhe,ukhe->uhqk', grad_wide, value_wide)
    delta_sum = lax.optimization_barrier(jnp.sum(probability * grad_probability, axis=-1, keepdims=True))
    grad_scores = (probability * (grad_probability - delta_sum) * scaling).astype(jnp.bfloat16)
    score_wide = grad_scores.astype(jnp.float32)
    weight_wide = probability_low.astype(jnp.float32)
    query_grad = jnp.einsum('uhqk,ukhe->uqhe', score_wide, key_wide)
    key_next = jnp.einsum('uhqk,uqhe->ukhe', score_wide[:, :, 1:], query_wide[:, 1:])
    value_next = jnp.einsum('uhqk,uqhe->ukhe', weight_wide[:, :, 1:], grad_wide[:, 1:])
    return (query_grad, key_next, value_next, grad_scores[:, :, 0], probability_low[:, :, 0])

def self_term(query_first, grad_first, score_first, weight_first, key_weight, value_weight):
    highest = lax.Precision.HIGHEST
    query_map = jnp.einsum('uhe,fhe->uhf', query_first.astype(jnp.float32), key_weight.astype(jnp.float32), precision=highest)
    grad_map = jnp.einsum('uhe,fhe->uhf', grad_first.astype(jnp.float32), value_weight.astype(jnp.float32), precision=highest)
    first = jnp.einsum('uhk,uhf->ukf', score_first.astype(jnp.float32), query_map, precision=highest)
    second = jnp.einsum('uhk,uhf->ukf', weight_first.astype(jnp.float32), grad_map, precision=highest)
    return first + second

def reference(queries, out_grad, states, gain, kv_weight, owners, slots):
    width = HEADS * HEAD_DIM
    flat_weight = kv_weight.reshape(D_ENC, 2 * width)
    key_weight = kv_weight[:, 0].reshape(D_ENC, HEADS, HEAD_DIM)
    value_weight = kv_weight[:, 1].reshape(D_ENC, HEADS, HEAD_DIM)

    def one_sequence(bundle):
        query_rows, grad_rows, state_rows, owner_ids, slot_ids = bundle
        values = state_rows.astype(jnp.float32)
        inverse = lax.rsqrt(lax.optimization_barrier(jnp.mean(values * values, axis=-1, keepdims=True)) + EPS)
        normed = (values * inverse * gain).astype(jnp.bfloat16)
        neighbour_ids = (owner_ids * NB_DEV + slot_ids).reshape(-1).astype(jnp.int32)
        picked = jnp.take(normed, neighbour_ids, axis=0)
        pairs = jnp.dot(picked.reshape(-1, D_ENC), flat_weight, preferred_element_type=jnp.float32).astype(jnp.bfloat16)
        pairs = pairs.reshape(GROUPS, RETR * NL, 2, HEADS, HEAD_DIM)
        query_block = jnp.pad(query_rows, ((1, GROUP - 1), (0, 0))).reshape(GROUPS + 1, GROUP, HEADS, HEAD_DIM)[1:]
        grad_block = jnp.pad(grad_rows, ((1, GROUP - 1), (0, 0))).reshape(GROUPS + 1, GROUP, HEADS, HEAD_DIM)[1:]
        query_grad, key_next, value_next, score_first, weight_first = block_backward(query_block, grad_block, pairs[:, :, 0], pairs[:, :, 1])
        query_grad = jnp.concatenate([jnp.zeros((GROUP, width), jnp.float32), query_grad.reshape(GROUPS * GROUP, width)], axis=0)[1:TOKENS + 1]
        next_pairs = jnp.stack([key_next, value_next], axis=2).astype(jnp.bfloat16).reshape(GROUPS * RETR * NL, 2 * width)
        next_part = lax.dot_general(next_pairs, flat_weight, (((1,), (1,)), ((), ())), preferred_element_type=jnp.float32)
        next_part = next_part.reshape(GROUPS, RETR * NL, D_ENC)
        own_part = self_term(query_block[:, 0], grad_block[:, 0], score_first, weight_first, key_weight, value_weight)
        picked_grad = (next_part + own_part).astype(jnp.bfloat16).reshape(GROUPS * RETR, NL, D_ENC)
        normed_grad = jax.ops.segment_sum(picked_grad.astype(jnp.float32), neighbour_ids, num_segments=NEIGHS)
        scaled = normed_grad * gain
        state_grad = (inverse * scaled - values * inverse * inverse * inverse * lax.optimization_barrier(jnp.mean(scaled * values, axis=-1, keepdims=True))).astype(jnp.bfloat16)
        gain_part = lax.optimization_barrier(jnp.sum(normed_grad * values * inverse, axis=(0, 1)))
        return (query_grad.astype(jnp.bfloat16), state_grad, gain_part)
    query_grad, state_grad, gain_parts = lax.map(one_sequence, (queries, out_grad, states, owners, slots))
    return (query_grad, state_grad, lax.optimization_barrier(jnp.sum(gain_parts, axis=0)))
```

```python
import functools
import math

import jax
import jax.numpy as jnp
from jax import lax
from jax.experimental import pallas as pl
from jax.experimental.pallas import tpu as pltpu
from jax.sharding import PartitionSpec as P

HEAD_DIM = 128
GROUP = 64
EPS = 1e-06
Y_SIZE = 4
CHUNKS = 2
CAP = 3

MESH = pl.DeviceIdType.MESH
VMEM = pltpu.VMEM
F32 = jnp.float32
BF16 = jnp.bfloat16


def one_hot(mask):
    return jnp.where(mask, 1.0, 0.0).astype(BF16)


class Place:
    def __init__(self, ny, nz):
        me = lax.axis_index("seq")
        self.ny, self.nz = ny, nz
        self.y = lax.div(me, nz)
        self.z = lax.rem(me, nz)
        self.up = self.at(self.y, lax.rem(self.z + 1, nz))
        self.down = self.at(self.y, lax.rem(self.z + nz - 1, nz))
        self.across = [lax.rem(self.y + j, ny) for j in range(1, ny)]

    def at(self, y, z):
        return {"seq": y * self.nz + z}


def greet(devices):
    barrier = pltpu.get_barrier_semaphore()
    for device in devices:
        pl.semaphore_signal(barrier, inc=1, device_id=device, device_id_type=MESH)
    pl.semaphore_wait(barrier, len(devices))


def remote(src, dst, send_sem, recv_sem, device):
    return pltpu.make_async_remote_copy(
        src_ref=src,
        dst_ref=dst,
        send_sem=send_sem,
        recv_sem=recv_sem,
        device_id=device,
        device_id_type=MESH,
    )


def fetch_kernel(
    ny, nz, states_ref, gain_ref, table_ref, pos_ref, mine_ref, tab_ref,
    ring, tabs, outs, recv, acc,
    ring_send, ring_recv, y_send, y_recv, tab_send, tab_recv,
):
    half = nz // 2
    place = Place(ny, nz)
    rows = states_ref.shape[0]
    part = rows // CHUNKS
    block = outs.shape[1] // ny
    y = place.y

    def ring_part(slot, way, chunk):
        return ring.at[slot, pl.ds(way * rows + chunk * part, part)]

    def forward(slot, way, chunk):
        far = isinstance(slot, int) and slot == half - 1
        first = isinstance(slot, int) and slot == 0
        src = ring_part(half - 1, 0, chunk) if first else ring_part(slot - 1, way, chunk)
        dst = ring_part(slot, 1, chunk) if far else ring_part(slot, way, chunk)
        return remote(
            src,
            dst,
            ring_send.at[slot, way, chunk],
            ring_recv.at[slot, way, chunk],
            place.down if way == 0 else place.up,
        )

    def across(slot, j):
        there = place.across[j]
        return remote(
            outs.at[slot, pl.ds(there * block, block)],
            recv.at[slot, pl.ds(y * block, block)],
            y_send.at[slot, j],
            y_recv.at[slot, j],
            place.at(there, place.z),
        )

    def table_copy(j):
        there = place.across[j]
        return remote(
            table_ref.at[there], tabs.at[y], tab_send.at[j], tab_recv.at[j], place.at(there, place.z)
        )

    values = states_ref[...].astype(F32)
    inverse = lax.rsqrt(jnp.mean(values * values, axis=-1, keepdims=True) + EPS)
    ring[half - 1, :rows] = (values * inverse * gain_ref[...]).astype(BF16)

    greet([place.up, place.down] + [place.at(there, place.z) for there in place.across])
    for chunk in range(CHUNKS):
        for way in range(2):
            forward(0, way, chunk).start()
    for j in range(ny - 1):
        table_copy(j).start()
    acc[...] = jnp.zeros_like(acc)
    tabs[pl.ds(y, 1)] = table_ref[pl.ds(y, 1)]
    for j in range(ny - 1):
        table_copy(j).wait()
    asked = tabs[0]
    for j in range(1, ny):
        asked = asked + tabs[j]
    tab_ref[...] = asked

    wide = outs.shape[1]

    def pick(slot):
        row = tab_ref[pl.ds(slot, 1), :wide]
        index = lax.broadcasted_iota(jnp.int32, (2 * rows, wide), 0) + 1
        select = one_hot(index == row)
        picked = lax.dot_general(
            select, ring[slot], (((0,), (0,)), ((), ())), preferred_element_type=F32
        ).astype(BF16)
        outs[slot] = picked
        for j in range(ny - 1):
            across(slot, j).start()
        recv[slot, pl.ds(y * block, block)] = outs[slot, pl.ds(y * block, block)]

    def take(slot):
        for j in range(ny - 1):
            across(slot, j).wait_recv()
        index = lax.broadcasted_iota(jnp.int32, (pos_ref.shape[0], wide), 1) + slot * wide
        placing = one_hot(index == pos_ref[...])
        acc[...] += jnp.dot(placing, recv[slot], preferred_element_type=F32)

    def near(slot, last):
        for chunk in range(CHUNKS):
            for way in range(2):
                forward(slot, way, chunk).wait_recv()
                if not last:
                    forward(slot + 1, way, chunk).start()
                elif way == chunk:
                    forward(half - 1, way, chunk).start()
        pick(slot)

    near(0, half == 2)
    if half > 2:

        @pl.loop(1, half - 2)
        def _(slot):
            near(slot, False)
            take(slot - 1)

        near(half - 2, True)
        take(half - 3)
    for way in range(2):
        forward(half - 1, way, way).wait_recv()
    pick(half - 1)
    take(half - 2)
    take(half - 1)
    mine_ref[...] = acc[...].astype(BF16)

    for way in range(2):
        forward(half - 1, way, way).wait_send()

    @pl.loop(0, half - 1)
    def _(slot):
        for way in range(2):
            for chunk in range(CHUNKS):
                remote(
                    ring_part(0, way, chunk),
                    ring_part(0, way, chunk),
                    ring_send.at[slot, way, chunk],
                    ring_recv.at[slot, way, chunk],
                    place.down if way == 0 else place.up,
                ).wait_send()

    @pl.loop(0, half)
    def _(slot):
        for j in range(ny - 1):
            across(slot, j).wait_send()


def fetch(ny, nz, states, gain, table, pos):
    half = nz // 2
    rows, width = states.shape
    wanted = pos.shape[0]
    block = 2 * CAP * 8
    return pl.pallas_call(
        functools.partial(fetch_kernel, ny, nz),
        out_shape=(
            jax.ShapeDtypeStruct((wanted, width), BF16),
            jax.ShapeDtypeStruct(table.shape[1:], jnp.int32),
        ),
        in_specs=[pl.BlockSpec(memory_space=VMEM)] * 4,
        out_specs=(pl.BlockSpec(memory_space=VMEM),) * 2,
        scratch_shapes=[
            VMEM((half, 2 * rows, width), BF16),
            VMEM(table.shape, jnp.int32),
            VMEM((half, ny * block, width), BF16),
            VMEM((half, ny * block, width), BF16),
            VMEM((wanted, width), F32),
            pltpu.SemaphoreType.DMA((half, 2, CHUNKS)),
            pltpu.SemaphoreType.DMA((half, 2, CHUNKS)),
            pltpu.SemaphoreType.DMA((half, ny - 1)),
            pltpu.SemaphoreType.DMA((half, ny - 1)),
            pltpu.SemaphoreType.DMA((ny - 1,)),
            pltpu.SemaphoreType.DMA((ny - 1,)),
        ],
        compiler_params=pltpu.CompilerParams(
            collective_id=1, has_side_effects=True, vmem_limit_bytes=40 << 20
        ),
        cost_estimate=pl.CostEstimate(flops=2 * 10**9, bytes_accessed=10**8, transcendentals=0),
    )(states, gain, table, pos)


def attend_kernel(
    pages_ref, group_ref, rgain_ref, q_ref, do_ref, wk_ref, wv_ref, dq_ref, grad_ref, gain_ref, acc
):
    step = pl.program_id(0)
    scaling = 1.0 / math.sqrt(HEAD_DIM)
    tokens, keys = q_ref.shape[0], pages_ref.shape[0]
    pages = pages_ref[...]
    key_all = jnp.dot(pages, wk_ref[...], preferred_element_type=F32).astype(BF16)
    value_all = jnp.dot(pages, wv_ref[...], preferred_element_type=F32).astype(BF16)
    mask = group_ref[...] == lax.div(lax.broadcasted_iota(jnp.int32, (tokens, keys), 1), GROUP)
    minor = (((1,), (1,)), ((), ()))
    major = (((0,), (0,)), ((), ()))
    key_grads, value_grads = [], []
    for head in range(q_ref.shape[1] // HEAD_DIM):
        columns = slice(head * HEAD_DIM, (head + 1) * HEAD_DIM)
        query, grad = q_ref[:, columns], do_ref[:, columns]
        key, value = key_all[:, columns], value_all[:, columns]
        scores = lax.dot_general(query, key, minor, preferred_element_type=F32) * scaling
        weights = jnp.where(mask, jnp.exp(jnp.where(mask, scores, 0.0)), 0.0)
        total = jnp.sum(weights, axis=-1, keepdims=True)
        probability = weights / jnp.where(total == 0.0, 1.0, total)
        grad_probability = lax.dot_general(grad, value, minor, preferred_element_type=F32)
        delta = jnp.sum(probability * grad_probability, axis=-1, keepdims=True)
        grad_scores = (probability * (grad_probability - delta) * scaling).astype(BF16)
        low = probability.astype(BF16)
        dq_ref[:, columns] = jnp.dot(grad_scores, key, preferred_element_type=F32).astype(BF16)
        key_grads.append(lax.dot_general(grad_scores, query, major, preferred_element_type=F32))
        value_grads.append(lax.dot_general(low, grad, major, preferred_element_type=F32))
    key_grad = jnp.concatenate(key_grads, axis=1).astype(BF16)
    value_grad = jnp.concatenate(value_grads, axis=1).astype(BF16)
    added = lax.dot_general(key_grad, wk_ref[...], minor, preferred_element_type=F32)
    added += lax.dot_general(value_grad, wv_ref[...], minor, preferred_element_type=F32)

    @pl.when(step == 0)
    def _():
        acc[...] = added

    @pl.when(step > 0)
    def _():
        acc[...] += added

    @pl.when(step == pl.num_programs(0) - 1)
    def _():
        picked_grad = acc[...].astype(BF16)
        grad_ref[...] = picked_grad
        products = picked_grad.astype(F32) * pages.astype(F32)
        gain_ref[...] = jnp.sum(products, axis=0, keepdims=True) * rgain_ref[...]


def attend(pages, group, rgain, queries, out_grad, weight):
    keys, enc = pages.shape
    tokens, width = queries.shape
    wide = 256
    steps = width // wide
    whole = lambda *shape: pl.BlockSpec(shape, lambda i: (0, 0))
    column = lambda rows, first: pl.BlockSpec((rows, wide), lambda i: (0, first + i))
    return pl.pallas_call(
        attend_kernel,
        grid=(steps,),
        out_shape=(
            jax.ShapeDtypeStruct((tokens, width), BF16),
            jax.ShapeDtypeStruct((keys, enc), BF16),
            jax.ShapeDtypeStruct((1, enc), F32),
        ),
        in_specs=[
            whole(keys, enc), whole(tokens, 1), whole(1, enc),
            column(tokens, 0), column(tokens, 0), column(enc, 0), column(enc, steps),
        ],
        out_specs=(column(tokens, 0), whole(keys, enc), whole(1, enc)),
        scratch_shapes=[VMEM((keys, enc), F32)],
        compiler_params=pltpu.CompilerParams(vmem_limit_bytes=32 << 20),
    )(pages, group, rgain, queries, out_grad, weight, weight)


def give_kernel(
    ny, nz, nb, grad_ref, pos_ref, tab_ref, states_ref, gain_ref, gain_part_ref, out_ref, gain_out_ref,
    outs, recv, sums_in, sums_out, added, own, by_batch, by_y, by_z,
    ring_send, ring_recv, y_send, y_recv, b_send, b_recv, gy_send, gy_recv, z_send, z_recv,
):
    half = nz // 2
    place = Place(ny, nz)
    y, z, b = place.y, place.z, lax.axis_index("batch")
    rows, width = states_ref.shape
    part = rows // CHUNKS
    wide = outs.shape[1]
    block = wide // ny
    b_peers = [lax.rem(b + j, nb) for j in range(1, nb)]
    z_peers = [lax.rem(z + j, nz) for j in range(1, nz)]

    def part_of(ref, slot, way, chunk):
        return ref.at[slot, pl.ds(way * rows + chunk * part, part)]

    def pass_on(distance, way, chunk):
        far = isinstance(distance, int) and distance == half
        return remote(
            part_of(sums_out, distance - 1, 1 if far else way, chunk),
            part_of(sums_in, distance - 1, way, chunk),
            ring_send.at[distance - 1, way, chunk],
            ring_recv.at[distance - 1, way, chunk],
            place.up if way == 0 else place.down,
        )

    def across(slot, j):
        there = place.across[j]
        return remote(
            outs.at[slot, pl.ds(there * block, block)],
            recv.at[slot, pl.ds(y * block, block)],
            y_send.at[slot, j],
            y_recv.at[slot, j],
            place.at(there, z),
        )

    def b_copy(j):
        return remote(
            by_batch.at[b], by_batch.at[b], b_send.at[j], b_recv.at[j], {"batch": b_peers[j]}
        )

    def gy_copy(j):
        return remote(
            by_y.at[y], by_y.at[y], gy_send.at[j], gy_recv.at[j], place.at(place.across[j], z)
        )

    def z_copy(j):
        return remote(
            by_z.at[z], by_z.at[z], z_send.at[j], z_recv.at[j], place.at(y, z_peers[j])
        )

    def total(ref):
        result = ref[0]
        for i in range(1, ref.shape[0]):
            result = result + ref[i]
        return result

    lanes = width // 128
    by_batch[pl.ds(b, 1)] = jnp.zeros_like(by_batch[pl.ds(b, 1)])
    for i in range(lanes):
        by_batch[b, i : i + 1] = gain_part_ref[:, i * 128 : (i + 1) * 128]

    greet(
        [{"batch": peer} for peer in b_peers]
        + [place.at(there, z) for there in place.across]
        + [place.at(y, there) for there in z_peers]
    )

    def scatter(slot):
        index = lax.broadcasted_iota(jnp.int32, (wide, pos_ref.shape[1]), 0) + slot * wide
        placing = one_hot(index == pos_ref[...])
        outs[slot] = jnp.dot(placing, grad_ref[...], preferred_element_type=F32).astype(BF16)
        for j in range(ny - 1):
            across(slot, j).start()
        recv[slot, pl.ds(y * block, block)] = outs[slot, pl.ds(y * block, block)]

    def gather(slot):
        for j in range(ny - 1):
            across(slot, j).wait_recv()
        row = tab_ref[pl.ds(slot, 1), :wide]
        index = lax.broadcasted_iota(jnp.int32, (2 * rows, wide), 0) + 1
        select = one_hot(index == row)
        added[...] = jnp.dot(select, recv[slot], preferred_element_type=F32)

    def chunk_rows(way, chunk):
        return pl.ds(way * rows + chunk * part, part)

    def relay(distance, first):
        gather(distance - 1)
        for chunk in range(CHUNKS):
            for way in range(2):
                here = chunk_rows(way, chunk)
                value = added[here]
                if not first or way == chunk:
                    pass_on(distance + 1, way, chunk).wait_recv()
                    value = value + sums_in[distance, here].astype(F32)
                sums_out[distance - 1, here] = value.astype(BF16)
                pass_on(distance, way, chunk).start()

    scatter(half - 1)
    for j in range(nb - 1):
        b_copy(j).start()
    if half > 1:
        scatter(half - 2)
    gather(half - 1)
    own[...] = added[:rows]
    sums_out[half - 1, pl.ds(rows, rows)] = added[pl.ds(rows, rows)].astype(BF16)
    for way in range(2):
        pass_on(half, way, way).start()
    if half > 2:
        scatter(half - 3)
    relay(half - 1, True)
    for j in range(nb - 1):
        b_copy(j).wait()
    by_y[y] = total(by_batch)
    for j in range(ny - 1):
        gy_copy(j).start()

    if half > 2:

        @pl.loop(0, half - 3)
        def _(i):
            distance = half - 2 - i
            scatter(distance - 2)
            relay(distance, False)

        for j in range(ny - 1):
            gy_copy(j).wait()
        by_z[z] = total(by_y)
        for j in range(nz - 1):
            z_copy(j).start()
        relay(1, False)
    else:
        for j in range(ny - 1):
            gy_copy(j).wait()
        by_z[z] = total(by_y)
        for j in range(nz - 1):
            z_copy(j).start()

    for j in range(nz - 1):
        z_copy(j).wait()
    result = total(by_z)
    for i in range(lanes):
        gain_out_ref[:, i * 128 : (i + 1) * 128] = result[i : i + 1]

    gain = gain_ref[...]
    for chunk in range(CHUNKS):
        here = pl.ds(chunk * part, part)
        for way in range(2):
            pass_on(1, way, chunk).wait_recv()
        normed_grad = own[here] + sums_in[0, here].astype(F32)
        normed_grad = normed_grad + sums_in[0, pl.ds(rows + chunk * part, part)].astype(F32)
        values = states_ref[here].astype(F32)
        inverse = lax.rsqrt(jnp.mean(values * values, axis=-1, keepdims=True) + EPS)
        scaled = normed_grad * gain
        inner = jnp.mean(scaled * values, axis=-1, keepdims=True)
        out_ref[here] = (
            inverse * scaled - values * (inverse * inverse * inverse * inner)
        ).astype(BF16)

    for way in range(2):
        pass_on(half, way, way).wait_send()

    @pl.loop(1, half)
    def _(distance):
        for way in range(2):
            for chunk in range(CHUNKS):
                pass_on(distance, way, chunk).wait_send()

    @pl.loop(0, half)
    def _(slot):
        for j in range(ny - 1):
            across(slot, j).wait_send()


def give(ny, nz, nb, grads, pos, tab, states, gain, gain_part):
    half = nz // 2
    rows, width = states.shape
    wide = ny * 2 * CAP * 8
    dma = pltpu.SemaphoreType.DMA
    return pl.pallas_call(
        functools.partial(give_kernel, ny, nz, nb),
        out_shape=(
            jax.ShapeDtypeStruct((rows, width), BF16),
            jax.ShapeDtypeStruct((1, width), F32),
        ),
        in_specs=[pl.BlockSpec(memory_space=VMEM)] * 6,
        out_specs=(pl.BlockSpec(memory_space=VMEM),) * 2,
        scratch_shapes=[
            VMEM((half, wide, width), BF16),
            VMEM((half, wide, width), BF16),
            VMEM((half, 2 * rows, width), BF16),
            VMEM((half, 2 * rows, width), BF16),
            VMEM((2 * rows, width), F32),
            VMEM((rows, width), F32),
            VMEM((nb, 8, 128), F32),
            VMEM((ny, 8, 128), F32),
            VMEM((nz, 8, 128), F32),
            dma((half, 2, CHUNKS)), dma((half, 2, CHUNKS)),
            dma((half, ny - 1)), dma((half, ny - 1)),
            dma((nb - 1,)), dma((nb - 1,)),
            dma((ny - 1,)), dma((ny - 1,)),
            dma((nz - 1,)), dma((nz - 1,)),
        ],
        compiler_params=pltpu.CompilerParams(
            collective_id=2, has_side_effects=True, vmem_limit_bytes=40 << 20
        ),
    )(grads, pos, tab, states, gain, gain_part)


def requests(owners, slots, ny, nz, held, length):
    half = nz // 2
    me = lax.axis_index("seq")
    y, z = me // nz, me % nz
    per_group = owners.shape[1]
    last = jnp.stack([owners[-1], slots[-1]])
    before = lax.ppermute(last, "seq", [(i, i + 1) for i in range(ny * nz - 1)])
    target = owners.reshape(-1)
    order = jnp.arange(target.shape[0], dtype=jnp.int32)
    earlier = (target[None, :] == target[:, None]) & (order[None, :] < order[:, None])
    rank = jnp.sum(earlier.astype(jnp.int32), axis=1)
    owner = jnp.concatenate([before[0], target])
    slot = jnp.concatenate([before[1], slots.reshape(-1)])
    rank = jnp.concatenate([jnp.full((per_group,), CAP - 1, jnp.int32), rank])
    valid = jnp.arange(owner.shape[0]) >= jnp.where(me == 0, per_group, 0)
    column, ahead = owner // nz, (owner % nz - z + nz) % nz
    way = jnp.where(ahead >= half, 1, 0)
    distance = jnp.where(ahead == 0, half, jnp.where(ahead > half, nz - ahead, ahead))
    piece = way * CAP + rank
    pieces = 2 * CAP
    place = ((distance - 1) * ny + column) * pieces + piece
    step_of = jnp.where(valid, column * half + distance - 1, -1)
    place = jnp.where(valid, place, -1)
    token = jnp.arange(length, dtype=jnp.int32)
    pos = jnp.where(place[:, None] >= 0, place[:, None] * length + token[None, :], -1).reshape(-1)
    lane = jnp.arange(ny * pieces * length, dtype=jnp.int32)
    lane_piece = jnp.where(lane // (pieces * length) == y, lane // length % pieces, -1)
    cell = jnp.arange(ny * half, dtype=jnp.int32)
    hit = (cell[:, None, None] == step_of[None, None, :]) & (
        lane_piece[None, :, None] == piece[None, None, :]
    )
    value = way * (held * length) + slot * length + 1
    found = jnp.sum(jnp.where(hit, value[None, None, :], 0), axis=-1)
    table = jnp.where(found > 0, found + lane[None, :] % length, 0).reshape(ny, half, -1)
    table = jnp.pad(table, ((0, 0), (0, max(0, 8 - half)), (0, -table.shape[2] % 128)))
    return pos, table


def on_device(ny, nz, nb, queries, out_grad, states, gain, kv_weight, owners, slots):
    held, length, enc = states.shape[1:]
    tokens, width = queries.shape[1:]
    me = lax.axis_index("seq")
    weight = lax.all_gather(kv_weight.reshape(-1, 2 * width), "batch", axis=0, tiled=True)
    pos, table = requests(owners[0], slots[0], ny, nz, held, length)
    rows = states.reshape(held * length, enc)
    gain_row = gain.reshape(1, enc)
    pages, tab = fetch(ny, nz, rows, gain_row, table, pos[:, None])
    token = jnp.arange(tokens, dtype=jnp.int32)
    group = (token + 1) // GROUP
    group = jnp.where((group == 0) & (me == 0), -1, group)[:, None]
    query_grad, grads, gain_part = attend(
        pages, group, 1.0 / gain_row, queries[0], out_grad[0], weight
    )
    state_grad, gain_grad = give(ny, nz, nb, grads, pos[None, :], tab, rows, gain_row, gain_part)
    return (
        query_grad[None],
        state_grad.reshape(1, held, length, enc),
        gain_grad.reshape(enc),
    )


def solution(mesh):
    ny = Y_SIZE
    nz = mesh.shape["seq"] // ny
    nb = mesh.shape["batch"]
    return jax.shard_map(
        functools.partial(on_device, ny, nz, nb),
        mesh=mesh,
        in_specs=(
            P("batch", "seq", None),
            P("batch", "seq", None),
            P("batch", "seq", None, None),
            P(),
            P("batch", None, None),
            P("batch", "seq", None),
            P("batch", "seq", None),
        ),
        out_specs=(P("batch", "seq", None), P("batch", "seq", None, None), P()),
        check_vma=False,
    )
```

```python
import functools
import math

import jax
import jax.numpy as jnp
from jax import lax
from jax.experimental import pallas as pl
from jax.experimental.pallas import tpu as pltpu
from jax.sharding import PartitionSpec as P

HEAD_DIM = 128
GROUP = 64
EPS = 1e-06
Y_SIZE = 4
CHUNKS = 2
X_CORES = 2
CAP = 3

MESH = pl.DeviceIdType.MESH
VMEM = pltpu.VMEM
F32 = jnp.float32
BF16 = jnp.bfloat16


def one_hot(mask):
    return jnp.where(mask, 1.0, 0.0).astype(BF16)


class Place:
    def __init__(self, ny, nz):
        me = lax.axis_index("seq")
        self.ny, self.nz = ny, nz
        self.y = lax.div(me, nz)
        self.z = lax.rem(me, nz)
        self.up = self.at(self.y, lax.rem(self.z + 1, nz))
        self.down = self.at(self.y, lax.rem(self.z + nz - 1, nz))
        self.across = [lax.rem(self.y + j, ny) for j in range(1, ny)]

    def at(self, y, z):
        return {"seq": y * self.nz + z}


def remote(src, dst, send_sem, recv_sem, device):
    return pltpu.make_async_remote_copy(
        src_ref=src,
        dst_ref=dst,
        send_sem=send_sem,
        recv_sem=recv_sem,
        device_id=device,
        device_id_type=MESH,
    )

MINOR = (((1,), (1,)), ((), ()))
MAJOR = (((0,), (0,)), ((), ()))


def iota(shape, dim):
    return lax.broadcasted_iota(jnp.int32, shape, dim)


def inverse_norm(values):
    return lax.rsqrt(jnp.mean(values * values, axis=-1, keepdims=True) + EPS)


def kernel(
    ny, nz, nb,
    q_ref, do_ref, states_ref, gain_ref, kv_ref, ids_ref,
    dq_ref, out_ref, gain_out_ref,
    ring, tabs, tab, pos, outs, recv, acc, mine, grad_rows, ids, ids_before, weight,
    back, sums_in, sums_out, added, own, by_batch, by_y, by_z,
    ring_send, ring_recv, y_send, y_recv, tab_send, tab_recv, id_send, id_recv, w_send, w_recv,
    sum_send, sum_recv, back_send, back_recv, b_send, b_recv, gy_send, gy_recv, z_send, z_recv,
):
    half = nz // 2
    place = Place(ny, nz)
    y, z, b = place.y, place.z, lax.axis_index("batch")
    me = y * nz + z
    rows, width = states_ref.shape
    part = rows // CHUNKS
    wide = outs.shape[1]
    block = wide // ny
    wanted = acc.shape[0]
    steps_pad = tab.shape[0]
    count = ny * nz
    following = {"seq": lax.rem(me + 1, count)}
    preceding = {"seq": lax.rem(me + count - 1, count)}
    b_peers = [lax.rem(b + j, nb) for j in range(1, nb)]
    z_peers = [lax.rem(z + j, nz) for j in range(1, nz)]
    core = lax.rem(b, X_CORES)
    right = lax.rem(b + X_CORES, nb)
    left = lax.rem(b + nb - X_CORES, nb)
    opposite = lax.rem(b + 2 * X_CORES, nb)
    sibling = b + 1 - 2 * core


    def ring_part(slot, way, chunk):
        return ring.at[slot, pl.ds(way * rows + chunk * part, part)]

    def forward(slot, way, chunk):
        far = isinstance(slot, int) and slot == half - 1
        first = isinstance(slot, int) and slot == 0
        src = ring_part(half - 1, 0, chunk) if first else ring_part(slot - 1, way, chunk)
        dst = ring_part(slot, 1, chunk) if far else ring_part(slot, way, chunk)
        return remote(
            src,
            dst,
            ring_send.at[slot, way, chunk],
            ring_recv.at[slot, way, chunk],
            place.down if way == 0 else place.up,
        )

    def exchange(into, send, arrived, slot, j):
        there = place.across[j]
        return remote(
            outs.at[slot, pl.ds(there * block, block)],
            into.at[slot, pl.ds(y * block, block)],
            send.at[slot, j],
            arrived.at[slot, j],
            place.at(there, z),
        )

    def across(slot, j):
        return exchange(recv, y_send, y_recv, slot, j)

    def return_across(slot, j):
        return exchange(back, back_send, back_recv, slot, j)

    def table_copy(j):
        there = place.across[j]
        return remote(
            tabs.at[ny + there], tabs.at[y], tab_send.at[j], tab_recv.at[j], place.at(there, z)
        )


    depth = kv_ref.shape[0]
    cut = (depth + 31) // 32 * 16
    weight_parts = ((0, cut), (cut, depth - cut))

    def weight_copy(channel, number):
        first, size = weight_parts[number]
        if channel == 2:
            shard, device = (left, right) if number == 0 else (right, left)
        else:
            shard = (b, b, None, b, left, right, opposite)[channel]
            device = (right, left, None, sibling, sibling, sibling, sibling)[channel]
        there = weight.at[pl.ds(pl.multiple_of(shard * depth + first, 16), size)]
        return remote(
            kv_ref.at[pl.ds(first, size)] if channel in (0, 1, 3) else there,
            there,
            w_send.at[channel, number],
            w_recv.at[channel, number],
            {"batch": device},
        )

    def weights_one():
        weight_copy(0, 0).wait_recv()
        weight_copy(2, 0).start()
        weight_copy(4, 0).start()
        weight_copy(1, 1).wait_recv()
        weight_copy(2, 1).start()
        weight_copy(5, 1).start()

    def weights_two():
        weight_copy(0, 1).wait_recv()
        weight_copy(4, 1).start()
        weight_copy(1, 0).wait_recv()
        weight_copy(5, 0).start()

    def weights_three():
        for number in range(2):
            weight_copy(2, number).wait_recv()
            weight_copy(6, number).start()


    def part_of(ref, slot, way, chunk):
        return ref.at[slot, pl.ds(way * rows + chunk * part, part)]

    def pass_on(distance, way, chunk):
        far = isinstance(distance, int) and distance == half
        return remote(
            part_of(sums_out, distance - 1, 1 if far else way, chunk),
            part_of(sums_in, distance - 1, way, chunk),
            sum_send.at[distance - 1, way, chunk],
            sum_recv.at[distance - 1, way, chunk],
            place.up if way == 0 else place.down,
        )


    def b_copy(j):
        return remote(
            by_batch.at[b], by_batch.at[b], b_send.at[j], b_recv.at[j], {"batch": b_peers[j]}
        )

    def gy_copy(j):
        return remote(
            by_y.at[y], by_y.at[y], gy_send.at[j], gy_recv.at[j], place.at(place.across[j], z)
        )

    def z_copy(j):
        return remote(
            by_z.at[z], by_z.at[z], z_send.at[j], z_recv.at[j], place.at(y, z_peers[j])
        )

    def total(ref):
        result = ref[0]
        for i in range(1, ref.shape[0]):
            result = result + ref[i]
        return result


    values = states_ref[...].astype(F32)
    ring[half - 1, :rows] = (values * inverse_norm(values) * gain_ref[...]).astype(BF16)
    ids[...] = jnp.zeros_like(ids)
    ids[: ids_ref.shape[0], : ids_ref.shape[1]] = ids_ref[...]

    barrier = pltpu.get_barrier_semaphore()
    peers = (
        [{"batch": peer} for peer in b_peers]
        + [place.at(there, z) for there in place.across]
        + [place.at(y, there) for there in z_peers]
        + [preceding]
    )
    for peer in peers:
        pl.semaphore_signal(barrier, inc=1, device_id=peer, device_id_type=MESH)
    pl.semaphore_wait(barrier, len(peers))

    ids_copy = remote(ids, ids_before, id_send, id_recv, following)
    ids_copy.start()
    for chunk in range(CHUNKS):
        for way in range(2):
            forward(0, way, chunk).start()
    for number in range(2):
        weight_copy(0, number).start()
        weight_copy(1, 1 - number).start()
    for number in range(2):
        weight_copy(3, number).start()
    acc[...] = jnp.zeros_like(acc)
    weight[pl.ds(pl.multiple_of(b * depth, 16), depth)] = kv_ref[...]


    pieces = 2 * CAP
    length = block // pieces
    own_count = ids_ref.shape[1]
    group = own_count // 2
    request_count = own_count + group
    ids_copy.wait()
    lane = iota(ids.shape, 1)
    merged = jnp.where(lane < own_count, ids[...], pltpu.roll(ids_before[...], group, 1))
    known = (lane < own_count) | ((lane < request_count) & (me > 0))
    owner = jnp.where(known, merged, -1)[0:1]
    slot_id = merged[1:2]
    lane = lane[0:1]
    rank = jnp.where(lane < own_count, 0, CAP - 1)
    wide_owner = jnp.broadcast_to(owner, ids.shape)
    for shift in range(1, 2 * group):
        other = pltpu.roll(wide_owner, shift, 1)[0:1]
        source = lane - shift
        same = (other == owner) & (source >= 0) & (source < group)
        rank = jnp.where(same & (lane >= group) & (lane < own_count), 1, rank)
    column = jnp.zeros_like(owner)
    for j in range(1, ny):
        column = column + jnp.where(owner >= j * nz, 1, 0)
    ahead = owner - column * nz - z
    ahead = jnp.where(ahead < 0, ahead + nz, ahead)
    way = jnp.where(ahead >= half, 1, 0)
    distance = jnp.where(ahead == 0, half, jnp.where(ahead > half, nz - ahead, ahead))
    piece = way * CAP + rank
    cell = jnp.where(owner >= 0, column * steps_pad + distance - 1, -1)
    number = jnp.where(owner >= 0, ((distance - 1) * ny + column) * pieces + piece, -1)
    value = way * rows + slot_id * length + 1

    table_rows, table_lanes = ny * steps_pad, tab.shape[1]
    lanes_of = (table_lanes, lane.shape[1])
    row = iota(lanes_of, 0) - y * block
    row_piece = jnp.where((row >= 0) & (row < block), lax.div(row, length), -1)
    chosen = jnp.where(row_piece == piece, value, 0).astype(F32).astype(BF16)
    cells = one_hot(iota((table_rows, lane.shape[1]), 0) == cell)
    found = lax.dot_general(cells, chosen, MINOR, preferred_element_type=F32).astype(jnp.int32)
    token = lax.rem(iota((table_rows, table_lanes), 1), length)
    table = jnp.where(found > 0, found + token, 0)
    for j in range(ny):
        tabs[ny + j] = table[j * steps_pad : (j + 1) * steps_pad]
    for j in range(ny - 1):
        table_copy(j).start()
    tabs[pl.ds(y, 1)] = tabs[pl.ds(ny + y, 1)]

    spread_of = (pos.shape[1], lane.shape[1])
    spread = one_hot(lax.div(iota(spread_of, 0), length) == iota(spread_of, 1))
    numbers = jnp.broadcast_to(number, ids.shape).astype(F32).astype(BF16)
    placed = lax.dot_general(numbers, spread, MINOR, preferred_element_type=F32).astype(jnp.int32)
    token = lax.rem(iota(placed.shape, 1), length)
    pos[...] = jnp.where(placed >= 0, placed * length + token, -1)

    for j in range(ny - 1):
        table_copy(j).wait()
    asked = tabs[0]
    for j in range(1, ny):
        asked = asked + tabs[j]
    tab[...] = asked


    def selected(slot):
        row = tab[pl.ds(slot, 1), :wide]
        return one_hot(iota((2 * rows, wide), 0) + 1 == row)

    def placing(slot):
        return one_hot(iota((wide, wanted), 0) + slot * wide == pos[0:1, :wanted])

    def pick(slot):
        outs[slot] = lax.dot_general(
            selected(slot), ring[slot], MAJOR, preferred_element_type=F32
        ).astype(BF16)
        for j in range(ny - 1):
            across(slot, j).start()
        recv[slot, pl.ds(y * block, block)] = outs[slot, pl.ds(y * block, block)]

    def take(slot):
        for j in range(ny - 1):
            across(slot, j).wait_recv()
        acc[...] += lax.dot_general(placing(slot), recv[slot], MAJOR, preferred_element_type=F32)

    def near(slot, last):
        for chunk in range(CHUNKS):
            for way in range(2):
                forward(slot, way, chunk).wait_recv()
                if not last:
                    forward(slot + 1, way, chunk).start()
                elif way == chunk:
                    forward(half - 1, way, chunk).start()
        pick(slot)

    services = {2: weights_one, 4: weights_two}
    near(0, half == 2)
    if half > 2:

        @pl.loop(1, half - 2)
        def _(slot):
            near(slot, False)
            take(slot - 1)
            for at, service in services.items():
                if at < half - 2:
                    pl.when(slot == at)(service)

        near(half - 2, True)
        take(half - 3)
    for at, service in services.items():
        if at >= half - 2:
            service()
    weights_three()
    for way in range(2):
        forward(half - 1, way, way).wait_recv()
    pick(half - 1)
    take(half - 2)
    for channel in range(3, 7):
        for number in range(2):
            weight_copy(channel, number).wait_recv()
    take(half - 1)
    mine[...] = acc[...].astype(BF16)

    for way in range(2):
        forward(half - 1, way, way).wait_send()

    @pl.loop(0, half - 1)
    def _(slot):
        for way in range(2):
            for chunk in range(CHUNKS):
                remote(
                    ring_part(0, way, chunk),
                    ring_part(0, way, chunk),
                    ring_send.at[slot, way, chunk],
                    ring_recv.at[slot, way, chunk],
                    place.down if way == 0 else place.up,
                ).wait_send()

    @pl.loop(0, half)
    def _(slot):
        for j in range(ny - 1):
            across(slot, j).wait_send()

    for channel in range(7):
        for number in range(2):
            weight_copy(channel, number).wait_send()


    tokens = q_ref.shape[0]
    scaling = 1.0 / math.sqrt(HEAD_DIM)
    turn = lax.div(iota((tokens, wanted), 0) + 1, GROUP)
    key_group = lax.div(iota((tokens, wanted), 1), GROUP)
    mask = lax.rem(turn + 2, 3) == key_group
    mask = mask & ((turn > 0) | (me > 0))
    pages = mine[...]
    heads_wide = 2 * HEAD_DIM
    steps = q_ref.shape[1] // heads_wide
    acc[...] = jnp.zeros_like(acc)

    @pl.loop(0, steps)
    def _(step):
        here = pl.ds(pl.multiple_of(step * heads_wide, heads_wide), heads_wide)
        there = pl.ds(
            pl.multiple_of((steps + step) * heads_wide, heads_wide), heads_wide
        )
        key_weight, value_weight = weight[:, here], weight[:, there]
        key_all = jnp.dot(pages, key_weight, preferred_element_type=F32).astype(BF16)
        value_all = jnp.dot(pages, value_weight, preferred_element_type=F32).astype(BF16)
        queries, grads = q_ref[:, here], do_ref[:, here]
        query_grads, key_grads, value_grads = [], [], []
        for head in range(heads_wide // HEAD_DIM):
            columns = slice(head * HEAD_DIM, (head + 1) * HEAD_DIM)
            query, grad = queries[:, columns], grads[:, columns]
            key, val = key_all[:, columns], value_all[:, columns]
            scores = lax.dot_general(query, key, MINOR, preferred_element_type=F32) * scaling
            weights = jnp.where(mask, jnp.exp(jnp.where(mask, scores, 0.0)), 0.0)
            over = jnp.sum(weights, axis=-1, keepdims=True)
            probability = weights / jnp.where(over == 0.0, 1.0, over)
            grad_probability = lax.dot_general(grad, val, MINOR, preferred_element_type=F32)
            delta = jnp.sum(probability * grad_probability, axis=-1, keepdims=True)
            grad_scores = (probability * (grad_probability - delta) * scaling).astype(BF16)
            low = probability.astype(BF16)
            query_grads.append(jnp.dot(grad_scores, key, preferred_element_type=F32))
            key_grads.append(lax.dot_general(grad_scores, query, MAJOR, preferred_element_type=F32))
            value_grads.append(lax.dot_general(low, grad, MAJOR, preferred_element_type=F32))
        dq_ref[:, here] = jnp.concatenate(query_grads, axis=1).astype(BF16)
        key_grad = jnp.concatenate(key_grads, axis=1).astype(BF16)
        value_grad = jnp.concatenate(value_grads, axis=1).astype(BF16)
        change = lax.dot_general(key_grad, key_weight, MINOR, preferred_element_type=F32)
        change += lax.dot_general(value_grad, value_weight, MINOR, preferred_element_type=F32)
        acc[...] += change

    grad_rows[...] = acc[...].astype(BF16)


    def scatter(slot):
        outs[slot] = jnp.dot(placing(slot), grad_rows[...], preferred_element_type=F32).astype(BF16)
        for j in range(ny - 1):
            return_across(slot, j).start()
        back[slot, pl.ds(y * block, block)] = outs[slot, pl.ds(y * block, block)]

    def gather(slot):
        for j in range(ny - 1):
            return_across(slot, j).wait_recv()
        added[...] = jnp.dot(selected(slot), back[slot], preferred_element_type=F32)

    def relay(distance, first):
        gather(distance - 1)
        for chunk in range(CHUNKS):
            for way in range(2):
                here = pl.ds(way * rows + chunk * part, part)
                total_here = added[here]
                if not first or way == chunk:
                    pass_on(distance + 1, way, chunk).wait_recv()
                    total_here = total_here + sums_in[distance, here].astype(F32)
                sums_out[distance - 1, here] = total_here.astype(BF16)
                pass_on(distance, way, chunk).start()

    def gain_one():
        lanes = width // 128
        products = jnp.sum(grad_rows[...].astype(F32) * mine[...].astype(F32), axis=0, keepdims=True)
        products = products / gain_ref[...]
        by_batch[pl.ds(b, 1)] = jnp.zeros_like(by_batch[pl.ds(b, 1)])
        for i in range(lanes):
            by_batch[b, i : i + 1] = products[:, i * 128 : (i + 1) * 128]
        for j in range(nb - 1):
            b_copy(j).start()

    def gain_two():
        for j in range(nb - 1):
            b_copy(j).wait()
        by_y[y] = total(by_batch)
        for j in range(ny - 1):
            gy_copy(j).start()

    def gain_three():
        for j in range(ny - 1):
            gy_copy(j).wait()
        by_z[z] = total(by_y)
        for j in range(nz - 1):
            z_copy(j).start()

    scatter(half - 1)
    scatter(half - 2)
    gather(half - 1)
    own[...] = added[:rows]
    sums_out[half - 1, pl.ds(rows, rows)] = added[pl.ds(rows, rows)].astype(BF16)
    for way in range(2):
        pass_on(half, way, way).start()
    gain_one()
    if half > 2:
        scatter(half - 3)
    relay(half - 1, True)
    gain_two()
    if half > 2:

        @pl.loop(0, half - 3)
        def _(i):
            distance = half - 2 - i
            scatter(distance - 2)
            relay(distance, False)

    gain_three()
    if half > 2:
        relay(1, False)

    for j in range(nz - 1):
        z_copy(j).wait()
    result = total(by_z)
    for i in range(width // 128):
        gain_out_ref[:, i * 128 : (i + 1) * 128] = result[i : i + 1]

    for chunk in range(CHUNKS):
        here = pl.ds(chunk * part, part)
        for way in range(2):
            pass_on(1, way, chunk).wait_recv()
        normed_grad = own[here] + sums_in[0, here].astype(F32)
        normed_grad = normed_grad + sums_in[0, pl.ds(rows + chunk * part, part)].astype(F32)
        values = states_ref[here].astype(F32)
        inverse = inverse_norm(values)
        scaled = normed_grad * gain_ref[...]
        inner = jnp.mean(scaled * values, axis=-1, keepdims=True)
        out_ref[here] = (
            inverse * scaled - values * (inverse * inverse * inverse * inner)
        ).astype(BF16)

    for way in range(2):
        pass_on(half, way, way).wait_send()

    @pl.loop(1, half)
    def _(distance):
        for way in range(2):
            for chunk in range(CHUNKS):
                pass_on(distance, way, chunk).wait_send()

    @pl.loop(0, half)
    def _(slot):
        for j in range(ny - 1):
            return_across(slot, j).wait_send()


def on_device(ny, nz, nb, queries, out_grad, states, gain, kv_weight, owners, slots):
    held, length, enc = states.shape[1:]
    tokens, width = queries.shape[1:]
    half, rows = nz // 2, held * length
    wanted = owners.shape[1] * owners.shape[2] * 3 // 2 * length
    wide = ny * 2 * CAP * length
    table = (max(8, half), wide + -wide % 128)
    ids = jnp.stack([owners.reshape(-1), slots.reshape(-1)])
    dma = pltpu.SemaphoreType.DMA
    query_grad, state_grad, gain_grad = pl.pallas_call(
        functools.partial(kernel, ny, nz, nb),
        out_shape=(
            jax.ShapeDtypeStruct((tokens, width), BF16),
            jax.ShapeDtypeStruct((rows, enc), BF16),
            jax.ShapeDtypeStruct((1, enc), F32),
        ),
        in_specs=[pl.BlockSpec(memory_space=VMEM)] * 6,
        out_specs=(pl.BlockSpec(memory_space=VMEM),) * 3,
        scratch_shapes=[
            VMEM((half, 2 * rows, enc), BF16),
            VMEM((2 * ny,) + table, jnp.int32),
            VMEM(table, jnp.int32),
            VMEM((8, wanted + -wanted % 128), jnp.int32),
            VMEM((half, wide, enc), BF16),
            VMEM((half, wide, enc), BF16),
            VMEM((wanted, enc), F32),
            VMEM((wanted, enc), BF16),
            VMEM((wanted, enc), BF16),
            VMEM((8, 128), jnp.int32),
            VMEM((8, 128), jnp.int32),
            VMEM((enc, 2 * width), BF16),
            VMEM((half, wide, enc), BF16),
            VMEM((half, 2 * rows, enc), BF16),
            VMEM((half, 2 * rows, enc), BF16),
            VMEM((2 * rows, enc), F32),
            VMEM((rows, enc), F32),
            VMEM((nb, 8, 128), F32),
            VMEM((ny, 8, 128), F32),
            VMEM((nz, 8, 128), F32),
            dma((half, 2, CHUNKS)), dma((half, 2, CHUNKS)),
            dma((half, ny - 1)), dma((half, ny - 1)),
            dma((ny - 1,)), dma((ny - 1,)),
            dma, dma,
            dma((7, 2)), dma((7, 2)),
            dma((half, 2, CHUNKS)), dma((half, 2, CHUNKS)),
            dma((half, ny - 1)), dma((half, ny - 1)),
            dma((nb - 1,)), dma((nb - 1,)),
            dma((ny - 1,)), dma((ny - 1,)),
            dma((nz - 1,)), dma((nz - 1,)),
        ],
        compiler_params=pltpu.CompilerParams(
            collective_id=1, has_side_effects=True, vmem_limit_bytes=48 << 20
        ),
    )(
        queries[0], out_grad[0], states.reshape(rows, enc), gain.reshape(1, enc),
        kv_weight.reshape(-1, 2 * width), ids,
    )
    return (
        query_grad[None],
        state_grad.reshape(1, held, length, enc),
        gain_grad.reshape(enc),
    )


def solution(mesh):
    ny = Y_SIZE
    nz = mesh.shape["seq"] // ny
    nb = mesh.shape["batch"]
    return jax.shard_map(
        functools.partial(on_device, ny, nz, nb),
        mesh=mesh,
        in_specs=(
            P("batch", "seq", None),
            P("batch", "seq", None),
            P("batch", "seq", None, None),
            P(),
            P("batch", None, None),
            P("batch", "seq", None),
            P("batch", "seq", None),
        ),
        out_specs=(P("batch", "seq", None), P("batch", "seq", None, None), P()),
        check_vma=False,
    )
```

```python
import functools
import math

import jax
import jax.numpy as jnp
from jax import lax
from jax.experimental import pallas as pl
from jax.experimental.pallas import tpu as pltpu
from jax.sharding import PartitionSpec as P

HEAD_DIM = 128
GROUP = 64
EPS = 1e-06
Y_SIZE = 4
CHUNKS = 2
X_CORES = 2
MAIN = 4
CAP = 3

MESH = pl.DeviceIdType.MESH
VMEM = pltpu.VMEM
F32 = jnp.float32
BF16 = jnp.bfloat16


def one_hot(mask):
    return jnp.where(mask, 1.0, 0.0).astype(BF16)


class Place:
    def __init__(self, ny, nz):
        me = lax.axis_index("seq")
        self.ny, self.nz = ny, nz
        self.y = lax.div(me, nz)
        self.z = lax.rem(me, nz)
        self.up = self.at(self.y, lax.rem(self.z + 1, nz))
        self.down = self.at(self.y, lax.rem(self.z + nz - 1, nz))
        order = sorted(range(1, ny), key=lambda j: -min(j, ny - j))
        self.across = [lax.rem(self.y + j, ny) for j in order]

    def at(self, y, z):
        return {"seq": y * self.nz + z}


def remote(src, dst, send_sem, recv_sem, device):
    return pltpu.make_async_remote_copy(
        src_ref=src,
        dst_ref=dst,
        send_sem=send_sem,
        recv_sem=recv_sem,
        device_id=device,
        device_id_type=MESH,
    )


MINOR = (((1,), (1,)), ((), ()))
MAJOR = (((0,), (0,)), ((), ()))


def iota(shape, dim):
    return lax.broadcasted_iota(jnp.int32, shape, dim)


def inverse_norm(values):
    return lax.rsqrt(jnp.mean(values * values, axis=-1, keepdims=True) + EPS)


def kernel(
    ny, nz, nb,
    q_hbm, do_hbm, states_ref, gain_ref, kv_hbm, owners_ref, slots_ref,
    dq_ref, out_ref, gain_out_ref,
    ring, tabs, tab, pos, outs, recv, acc, mine, grad_rows, ids, ids_before, weight,
    back, sums_in, sums_out, added, own, by_batch, by_y, by_z, q_ref, do_ref, kv_ref,
    ring_send, ring_recv, y_send, y_recv, tab_send, tab_recv, id_send, id_recv, w_send, w_recv,
    sum_send, sum_recv, back_send, back_recv, b_send, b_recv, gy_send, gy_recv, z_send, z_recv,
    in_sems,
):
    half = nz // 2
    place = Place(ny, nz)
    y, z, b = place.y, place.z, lax.axis_index("batch")
    me = y * nz + z
    rows, width = states_ref.shape
    part = rows // CHUNKS
    wide = outs.shape[1]
    block = wide // ny
    wanted = acc.shape[0]
    pieces = 2 * CAP
    length = block // pieces
    steps_pad = tab.shape[0]
    count = ny * nz
    following = {"seq": lax.rem(me + 1, count)}
    preceding = {"seq": lax.rem(me + count - 1, count)}
    b_peers = [lax.rem(b + j, nb) for j in range(1, nb)]
    z_peers = [lax.rem(z + j, nz) for j in range(1, nz)]
    core = lax.rem(b, X_CORES)
    right = lax.rem(b + X_CORES, nb)
    left = lax.rem(b + nb - X_CORES, nb)
    opposite = lax.rem(b + 2 * X_CORES, nb)
    sibling = b + 1 - 2 * core


    def ring_part(slot, way, chunk):
        return ring.at[slot, pl.ds(way * rows + chunk * part, part)]

    def forward(slot, way, chunk):
        far = isinstance(slot, int) and slot == half - 1
        first = isinstance(slot, int) and slot == 0
        src = ring_part(half - 1, 0, chunk) if first else ring_part(slot - 1, way, chunk)
        dst = ring_part(slot, 1, chunk) if far else ring_part(slot, way, chunk)
        return remote(
            src,
            dst,
            ring_send.at[slot, way, chunk],
            ring_recv.at[slot, way, chunk],
            place.down if way == 0 else place.up,
        )


    main, rest = MAIN * length, block - MAIN * length

    def exchange(into, send, arrived, slot, j):
        there = place.across[j]
        first, size, row = 0, block, slot
        if isinstance(slot, int) and slot == half - 1:
            size = main
        elif isinstance(slot, int) and slot == half:
            first, size, row = ny * main, rest, half - 1
        return remote(
            outs.at[row, pl.ds(first + there * size, size)],
            into.at[row, pl.ds(first + y * size, size)],
            send.at[slot, j],
            arrived.at[slot, j],
            place.at(there, z),
        )

    def keep(into, slot):
        if isinstance(slot, int) and slot == half - 1:
            here = pl.ds(y * main, main)
            into[half - 1, here] = outs[half - 1, here]
        elif isinstance(slot, int) and slot == half:
            here = pl.ds(ny * main + y * rest, rest)
            into[half - 1, here] = outs[half - 1, here]
        else:
            here = pl.ds(y * block, block)
            into[slot, here] = outs[slot, here]

    def across(slot, j):
        return exchange(recv, y_send, y_recv, slot, j)

    def return_across(slot, j):
        return exchange(back, back_send, back_recv, slot, j)

    def table_copy(j):
        there = place.across[j]
        return remote(
            tabs.at[ny + there], tabs.at[y], tab_send.at[j], tab_recv.at[j], place.at(there, z)
        )


    depth = kv_hbm.shape[0]
    cut = (depth + 31) // 32 * 16
    weight_parts = ((0, cut), (cut, depth - cut))

    def weight_copy(channel, number):
        first, size = weight_parts[number]
        if channel == 2:
            shard, device = (left, right) if number == 0 else (right, left)
        else:
            shard = (b, b, None, b, left, right, opposite)[channel]
            device = (right, left, None, sibling, sibling, sibling, sibling)[channel]
        there = weight.at[pl.ds(pl.multiple_of(shard * depth + first, 16), size)]
        return remote(
            there,
            there,
            w_send.at[channel, number],
            w_recv.at[channel, number],
            {"batch": device},
        )

    def weights_one():
        weight_copy(0, 0).wait_recv()
        weight_copy(2, 0).start()
        weight_copy(4, 0).start()
        weight_copy(1, 1).wait_recv()
        weight_copy(2, 1).start()
        weight_copy(5, 1).start()

    def weights_two():
        weight_copy(0, 1).wait_recv()
        weight_copy(4, 1).start()
        weight_copy(1, 0).wait_recv()
        weight_copy(5, 0).start()

    def weights_three():
        for number in range(2):
            weight_copy(2, number).wait_recv()
            weight_copy(6, number).start()


    def part_of(ref, slot, way, chunk):
        return ref.at[slot, pl.ds(way * rows + chunk * part, part)]

    def pass_on(distance, way, chunk):
        far = isinstance(distance, int) and distance == half
        return remote(
            part_of(sums_out, distance - 1, 1 if far else way, chunk),
            part_of(sums_in, distance - 1, way, chunk),
            sum_send.at[distance - 1, way, chunk],
            sum_recv.at[distance - 1, way, chunk],
            place.up if way == 0 else place.down,
        )


    def b_copy(j):
        return remote(
            by_batch.at[b], by_batch.at[b], b_send.at[j], b_recv.at[j], {"batch": b_peers[j]}
        )

    def gy_copy(j):
        return remote(
            by_y.at[y], by_y.at[y], gy_send.at[j], gy_recv.at[j], place.at(place.across[j], z)
        )

    def z_copy(j):
        return remote(
            by_z.at[z], by_z.at[z], z_send.at[j], z_recv.at[j], place.at(y, z_peers[j])
        )

    def total(ref):
        result = ref[0]
        for i in range(1, ref.shape[0]):
            result = result + ref[i]
        return result


    kv_in = pltpu.make_async_copy(kv_hbm, kv_ref, in_sems.at[0])
    q_in = pltpu.make_async_copy(q_hbm, q_ref, in_sems.at[1])
    do_in = pltpu.make_async_copy(do_hbm, do_ref, in_sems.at[2])
    for copy in (kv_in, q_in, do_in):
        copy.start()

    gain = gain_ref[...].reshape(1, width)
    values = states_ref[...].astype(F32)
    ring[half - 1, :rows] = (values * inverse_norm(values) * gain).astype(BF16)
    ids[...] = jnp.zeros_like(ids)
    group = owners_ref.shape[2]
    for i in range(owners_ref.shape[1]):
        ids[0:1, i * group : (i + 1) * group] = owners_ref[0, i : i + 1]
        ids[1:2, i * group : (i + 1) * group] = slots_ref[0, i : i + 1]

    barrier = pltpu.get_barrier_semaphore()
    peers = (
        [{"batch": peer} for peer in b_peers]
        + [place.at(there, z) for there in place.across]
        + [place.at(y, there) for there in z_peers]
        + [preceding]
    )
    for peer in peers:
        pl.semaphore_signal(barrier, inc=1, device_id=peer, device_id_type=MESH)
    pl.semaphore_wait(barrier, len(peers))

    ids_copy = remote(ids, ids_before, id_send, id_recv, following)
    ids_copy.start()
    for chunk in range(CHUNKS):
        for way in range(2):
            forward(0, way, chunk).start()


    own_count = 2 * group
    request_count = own_count + group
    ids_copy.wait()
    lane = iota(ids.shape, 1)
    merged = jnp.where(lane < own_count, ids[...], pltpu.roll(ids_before[...], group, 1))
    known = (lane < own_count) | ((lane < request_count) & (me > 0))
    owner = jnp.where(known, merged, -1)[0:1]
    slot_id = merged[1:2]
    lane = lane[0:1]
    rank = jnp.where(lane < own_count, 0, CAP - 1)
    wide_owner = jnp.broadcast_to(owner, ids.shape)
    for shift in range(1, 2 * group):
        other = pltpu.roll(wide_owner, shift, 1)[0:1]
        source = lane - shift
        same = (other == owner) & (source >= 0) & (source < group)
        rank = jnp.where(same & (lane >= group) & (lane < own_count), 1, rank)
    column = jnp.zeros_like(owner)
    for j in range(1, ny):
        column = column + jnp.where(owner >= j * nz, 1, 0)
    ahead = owner - column * nz - z
    ahead = jnp.where(ahead < 0, ahead + nz, ahead)
    way = jnp.where(ahead >= half, 1, 0)
    distance = jnp.where(ahead == 0, half, jnp.where(ahead > half, nz - ahead, ahead))
    piece = (1 - way) * CAP + rank
    cell = jnp.where(owner >= 0, column * steps_pad + distance - 1, -1)
    last = jnp.where(
        piece < MAIN, column * MAIN + piece, ny * MAIN + column * (pieces - MAIN) + piece - MAIN
    )
    number = jnp.where(distance == half, last, column * pieces + piece)
    number = jnp.where(owner >= 0, (distance - 1) * ny * pieces + number, -1)
    value = way * rows + slot_id * length + 1

    table_rows, table_lanes = ny * steps_pad, tab.shape[1]
    lanes_of = (table_lanes, lane.shape[1])
    cells = one_hot(iota((table_rows, lane.shape[1]), 0) == cell)

    def found_at(first, size, first_piece):
        row = iota(lanes_of, 0) - (first + y * size)
        inside = (row >= 0) & (row < size)
        return jnp.where(inside, lax.div(row, length) + first_piece, -1)

    def found_by(row_piece):
        chosen = jnp.where(row_piece == piece, value, 0).astype(F32).astype(BF16)
        return lax.dot_general(cells, chosen, MINOR, preferred_element_type=F32)

    whole = found_by(found_at(0, block, 0))
    cut_in_two = found_by(
        jnp.maximum(found_at(0, main, 0), found_at(ny * main, rest, MAIN))
    )
    step_of = lax.rem(iota((table_rows, table_lanes), 0), steps_pad)
    found = jnp.where(step_of == half - 1, cut_in_two, whole).astype(jnp.int32)
    token = lax.rem(iota((table_rows, table_lanes), 1), length)
    table = jnp.where(found > 0, found + token, 0)
    for j in range(ny):
        tabs[ny + j] = table[j * steps_pad : (j + 1) * steps_pad]
    for j in range(ny - 1):
        table_copy(j).start()
    tabs[pl.ds(y, 1)] = tabs[pl.ds(ny + y, 1)]

    spread_of = (pos.shape[1], lane.shape[1])
    spread = one_hot(lax.div(iota(spread_of, 0), length) == iota(spread_of, 1))
    numbers = jnp.broadcast_to(number, ids.shape).astype(F32).astype(BF16)
    placed = lax.dot_general(numbers, spread, MINOR, preferred_element_type=F32).astype(jnp.int32)
    token = lax.rem(iota(placed.shape, 1), length)
    pos[...] = jnp.where(placed >= 0, placed * length + token, -1)

    acc[...] = jnp.zeros_like(acc)
    kv_in.wait()
    own_shard = pl.ds(pl.multiple_of(b * depth, 16), depth)
    weight[own_shard, : kv_ref.shape[2]] = kv_ref[:, 0, :]
    weight[own_shard, kv_ref.shape[2] :] = kv_ref[:, 1, :]
    for number in range(2):
        weight_copy(0, number).start()
        weight_copy(1, 1 - number).start()
    for number in range(2):
        weight_copy(3, number).start()


    def selected_in(rows_there, first, size):
        row = tab[half - 1 : half, first : first + size]
        return one_hot(iota((rows_there, size), 0) + 1 == row)

    def selected(slot):
        row = tab[pl.ds(slot, 1), :wide]
        return one_hot(iota((2 * rows, wide), 0) + 1 == row)

    def placing(slot):
        return one_hot(iota((wide, wanted), 0) + slot * wide == pos[0:1, :wanted])

    def pick_by(select, shards):
        return lax.dot_general(select, shards, MAJOR, preferred_element_type=F32).astype(BF16)

    def pick(slot):
        if isinstance(slot, int) and slot == half:
            outs[half - 1, ny * main :] = pick_by(
                selected_in(rows, ny * main, ny * rest), ring[half - 1, :rows]
            )
        elif isinstance(slot, int) and slot == half - 1:
            outs[half - 1, : ny * main] = pick_by(
                selected_in(2 * rows, 0, ny * main), ring[half - 1]
            )
        else:
            outs[slot] = pick_by(selected(slot), ring[slot])
        for j in range(ny - 1):
            across(slot, j).start()
        keep(recv, slot)

    def take(slot):
        for j in range(ny - 1):
            across(slot, j).wait_recv()
            if isinstance(slot, int) and slot == half - 1:
                across(half, j).wait_recv()
        acc[...] += lax.dot_general(placing(slot), recv[slot], MAJOR, preferred_element_type=F32)

    def near(slot, last):
        hand_on(slot, last)
        pick(slot)

    def hand_on(slot, last):
        for chunk in range(CHUNKS):
            for way in range(2):
                forward(slot, way, chunk).wait_recv()
                if not last:
                    forward(slot + 1, way, chunk).start()
                elif way == chunk:
                    forward(half - 1, way, chunk).start()

    services = {2: weights_one, 4: weights_two}
    hand_on(0, half == 2)
    for j in range(ny - 1):
        table_copy(j).wait()
    asked = tabs[0]
    for j in range(1, ny):
        asked = asked + tabs[j]
    tab[...] = asked
    pick(half)
    pick(0)
    if half > 2:

        @pl.loop(1, half - 2)
        def _(slot):
            near(slot, False)
            take(slot - 1)
            for at, service in services.items():
                if at < half - 2:
                    pl.when(slot == at)(service)

        near(half - 2, True)
        take(half - 3)
    for at, service in services.items():
        if at >= half - 2:
            service()
    weights_three()
    for way in range(2):
        forward(half - 1, way, way).wait_recv()
    pick(half - 1)
    take(half - 2)
    for channel in range(3, 7):
        for number in range(2):
            weight_copy(channel, number).wait_recv()
    take(half - 1)
    mine[...] = acc[...].astype(BF16)

    for way in range(2):
        forward(half - 1, way, way).wait_send()

    @pl.loop(0, half - 1)
    def _(slot):
        for way in range(2):
            for chunk in range(CHUNKS):
                remote(
                    ring_part(0, way, chunk),
                    ring_part(0, way, chunk),
                    ring_send.at[slot, way, chunk],
                    ring_recv.at[slot, way, chunk],
                    place.down if way == 0 else place.up,
                ).wait_send()

    @pl.loop(0, half - 1)
    def _(slot):
        for j in range(ny - 1):
            across(slot, j).wait_send()

    for slot in (half - 1, half):
        for j in range(ny - 1):
            across(slot, j).wait_send()

    for channel in range(7):
        for number in range(2):
            weight_copy(channel, number).wait_send()


    q_in.wait()
    do_in.wait()
    tokens = q_ref.shape[0]
    scaling = 1.0 / math.sqrt(HEAD_DIM)
    turn = lax.div(iota((wanted, tokens), 1) + 1, GROUP)
    key_group = lax.div(iota((wanted, tokens), 0), GROUP)
    mask = lax.rem(turn + 2, 3) == key_group
    mask = mask & ((turn > 0) | (me > 0))
    pages = mine[...]
    heads_wide = min(8 * HEAD_DIM, q_ref.shape[1])
    steps = q_ref.shape[1] // heads_wide
    acc[...] = jnp.zeros_like(acc)

    @pl.loop(0, steps)
    def _(step):
        here = pl.ds(pl.multiple_of(step * heads_wide, heads_wide), heads_wide)
        there = pl.ds(
            pl.multiple_of((steps + step) * heads_wide, heads_wide), heads_wide
        )
        key_weight, value_weight = weight[:, here], weight[:, there]
        key_all = jnp.dot(pages, key_weight, preferred_element_type=F32).astype(BF16)
        value_all = jnp.dot(pages, value_weight, preferred_element_type=F32).astype(BF16)
        queries, grads = q_ref[:, here], do_ref[:, here]
        query_grads, key_grads, value_grads = [], [], []
        for head in range(heads_wide // HEAD_DIM):
            columns = slice(head * HEAD_DIM, (head + 1) * HEAD_DIM)
            query, grad = queries[:, columns], grads[:, columns]
            key, val = key_all[:, columns], value_all[:, columns]
            scores = lax.dot_general(key, query, MINOR, preferred_element_type=F32) * scaling
            weights = jnp.where(mask, jnp.exp(scores), 0.0)
            over = jnp.sum(weights, axis=0, keepdims=True)
            probability = weights * (1.0 / jnp.where(over == 0.0, 1.0, over))
            grad_probability = lax.dot_general(val, grad, MINOR, preferred_element_type=F32)
            delta = jnp.sum(probability * grad_probability, axis=0, keepdims=True)
            grad_scores = (probability * (grad_probability - delta) * scaling).astype(BF16)
            low = probability.astype(BF16)
            query_grads.append(lax.dot_general(grad_scores, key, MAJOR, preferred_element_type=F32))
            key_grads.append(jnp.dot(grad_scores, query, preferred_element_type=F32))
            value_grads.append(jnp.dot(low, grad, preferred_element_type=F32))
        dq_ref[:, here] = jnp.concatenate(query_grads, axis=1).astype(BF16)
        key_grad = jnp.concatenate(key_grads, axis=1).astype(BF16)
        value_grad = jnp.concatenate(value_grads, axis=1).astype(BF16)
        change = lax.dot_general(key_grad, key_weight, MINOR, preferred_element_type=F32)
        change += lax.dot_general(value_grad, value_weight, MINOR, preferred_element_type=F32)
        acc[...] += change

    grad_rows[...] = acc[...].astype(BF16)


    def scatter(slot):
        outs[slot] = jnp.dot(placing(slot), grad_rows[...], preferred_element_type=F32).astype(BF16)
        for j in range(ny - 1):
            return_across(slot, j).start()
        keep(back, slot)

    def scatter_rest():
        for j in range(ny - 1):
            return_across(half, j).start()
        keep(back, half)

    def gather_by(select, blocks):
        return jnp.dot(select, blocks, preferred_element_type=F32)

    def gather(slot):
        for j in range(ny - 1):
            return_across(slot, j).wait_recv()
        added[...] = gather_by(selected(slot), back[slot])

    def gather_far():
        for j in range(ny - 1):
            return_across(half - 1, j).wait_recv()
        added[...] = gather_by(
            selected_in(2 * rows, 0, ny * main), back[half - 1, : ny * main]
        )

    def gather_rest():
        for j in range(ny - 1):
            return_across(half, j).wait_recv()
        own[...] += gather_by(
            selected_in(rows, ny * main, ny * rest), back[half - 1, ny * main :]
        )

    def relay(distance, first):
        gather(distance - 1)
        for chunk in range(CHUNKS):
            for way in range(2):
                here = pl.ds(way * rows + chunk * part, part)
                total_here = added[here]
                if not first or way == chunk:
                    pass_on(distance + 1, way, chunk).wait_recv()
                    total_here = total_here + sums_in[distance, here].astype(F32)
                sums_out[distance - 1, here] = total_here.astype(BF16)
                pass_on(distance, way, chunk).start()

    def gain_one():
        lanes = width // 128
        products = jnp.sum(grad_rows[...].astype(F32) * mine[...].astype(F32), axis=0, keepdims=True)
        products = products / gain
        by_batch[pl.ds(b, 1)] = jnp.zeros_like(by_batch[pl.ds(b, 1)])
        for i in range(lanes):
            by_batch[b, i : i + 1] = products[:, i * 128 : (i + 1) * 128]
        for j in range(nb - 1):
            b_copy(j).start()

    def gain_two():
        for j in range(nb - 1):
            b_copy(j).wait()
        by_y[y] = total(by_batch)
        for j in range(ny - 1):
            gy_copy(j).start()

    def gain_three():
        for j in range(ny - 1):
            gy_copy(j).wait()
        by_z[z] = total(by_y)
        for j in range(nz - 1):
            z_copy(j).start()

    scatter(half - 1)
    scatter(half - 2)
    scatter_rest()
    gain_one()
    if half > 2:
        scatter(half - 3)
    gather_far()
    sums_out[half - 1, pl.ds(rows, rows)] = added[pl.ds(rows, rows)].astype(BF16)
    for way in range(2):
        pass_on(half, way, way).start()
    own[...] = added[:rows]
    gather_rest()
    relay(half - 1, True)
    gain_two()
    if half > 2:

        @pl.loop(0, half - 3)
        def _(i):
            distance = half - 2 - i
            scatter(distance - 2)
            relay(distance, False)

    gain_three()
    if half > 2:
        relay(1, False)

    for j in range(nz - 1):
        z_copy(j).wait()
    result = total(by_z)
    for i in range(width // 128):
        gain_out_ref[i * 128 : (i + 1) * 128] = result[i]

    for chunk in range(CHUNKS):
        here = pl.ds(chunk * part, part)
        for way in range(2):
            pass_on(1, way, chunk).wait_recv()
        normed_grad = own[here] + sums_in[0, here].astype(F32)
        normed_grad = normed_grad + sums_in[0, pl.ds(rows + chunk * part, part)].astype(F32)
        values = states_ref[here].astype(F32)
        inverse = inverse_norm(values)
        scaled = normed_grad * gain
        inner = jnp.mean(scaled * values, axis=-1, keepdims=True)
        out_ref[here] = (
            inverse * scaled - values * (inverse * inverse * inverse * inner)
        ).astype(BF16)

    for way in range(2):
        pass_on(half, way, way).wait_send()

    @pl.loop(1, half)
    def _(distance):
        for way in range(2):
            for chunk in range(CHUNKS):
                pass_on(distance, way, chunk).wait_send()

    @pl.loop(0, half - 1)
    def _(slot):
        for j in range(ny - 1):
            return_across(slot, j).wait_send()

    for slot in (half - 1, half):
        for j in range(ny - 1):
            return_across(slot, j).wait_send()


def on_device(ny, nz, nb, queries, out_grad, states, gain, kv_weight, owners, slots):
    held, length, enc = states.shape[1:]
    tokens, width = queries.shape[1:]
    half, rows = nz // 2, held * length
    wanted = owners.shape[1] * owners.shape[2] * 3 // 2 * length
    wide = ny * 2 * CAP * length
    table = (max(8, half), wide + -wide % 128)
    dma = pltpu.SemaphoreType.DMA
    query_grad, state_grad, gain_grad = pl.pallas_call(
        functools.partial(kernel, ny, nz, nb),
        out_shape=(
            jax.ShapeDtypeStruct((tokens, width), BF16),
            jax.ShapeDtypeStruct((rows, enc), BF16),
            jax.ShapeDtypeStruct((enc,), F32),
        ),
        in_specs=[
            pl.BlockSpec(memory_space=VMEM if inside else pl.ANY)
            for inside in (False, False, True, True, False, True, True)
        ],
        out_specs=(pl.BlockSpec(memory_space=VMEM),) * 3,
        scratch_shapes=[
            VMEM((half, 2 * rows, enc), BF16),
            VMEM((2 * ny,) + table, jnp.int32),
            VMEM(table, jnp.int32),
            VMEM((8, wanted + -wanted % 128), jnp.int32),
            VMEM((half, wide, enc), BF16),
            VMEM((half, wide, enc), BF16),
            VMEM((wanted, enc), F32),
            VMEM((wanted, enc), BF16),
            VMEM((wanted, enc), BF16),
            VMEM((8, 128), jnp.int32),
            VMEM((8, 128), jnp.int32),
            VMEM((enc, 2 * width), BF16),
            VMEM((half, wide, enc), BF16),
            VMEM((half, 2 * rows, enc), BF16),
            VMEM((half, 2 * rows, enc), BF16),
            VMEM((2 * rows, enc), F32),
            VMEM((rows, enc), F32),
            VMEM((nb, 8, 128), F32),
            VMEM((ny, 8, 128), F32),
            VMEM((nz, 8, 128), F32),
            VMEM((tokens, width), BF16),
            VMEM((tokens, width), BF16),
            VMEM(kv_weight.shape, BF16),
            dma((half, 2, CHUNKS)), dma((half, 2, CHUNKS)),
            dma((half + 1, ny - 1)), dma((half + 1, ny - 1)),
            dma((ny - 1,)), dma((ny - 1,)),
            dma, dma,
            dma((7, 2)), dma((7, 2)),
            dma((half, 2, CHUNKS)), dma((half, 2, CHUNKS)),
            dma((half + 1, ny - 1)), dma((half + 1, ny - 1)),
            dma((nb - 1,)), dma((nb - 1,)),
            dma((ny - 1,)), dma((ny - 1,)),
            dma((nz - 1,)), dma((nz - 1,)),
            dma((3,)),
        ],
        compiler_params=pltpu.CompilerParams(
            collective_id=1, has_side_effects=True, vmem_limit_bytes=54 << 20
        ),
    )(
        queries[0], out_grad[0], states.reshape(rows, enc), gain, kv_weight, owners, slots,
    )
    return (
        query_grad[None],
        state_grad.reshape(1, held, length, enc),
        gain_grad,
    )


def solution(mesh):
    ny = Y_SIZE
    nz = mesh.shape["seq"] // ny
    nb = mesh.shape["batch"]
    return jax.shard_map(
        functools.partial(on_device, ny, nz, nb),
        mesh=mesh,
        in_specs=(
            P("batch", "seq", None),
            P("batch", "seq", None),
            P("batch", "seq", None, None),
            P(),
            P("batch", None, None),
            P("batch", "seq", None),
            P("batch", "seq", None),
        ),
        out_specs=(P("batch", "seq", None), P("batch", "seq", None, None), P()),
        check_vma=False,
    )
```

```python
import functools
import math

import jax
import jax.numpy as jnp
from jax import lax
from jax.experimental import pallas as pl
from jax.experimental.pallas import tpu as pltpu
from jax.sharding import PartitionSpec as P

HEAD_DIM = 128
GROUP = 64
EPS = 1e-06
Y_SIZE = 4
CHUNKS = 2
X_CORES = 2
MAIN = 4
CAP = 3

MESH = pl.DeviceIdType.MESH
VMEM = pltpu.VMEM
F32 = jnp.float32
BF16 = jnp.bfloat16


def one_hot(mask):
    return jnp.where(mask, 1.0, 0.0).astype(BF16)


class Place:
    def __init__(self, ny, nz):
        me = lax.axis_index("seq")
        self.ny, self.nz = ny, nz
        self.y = lax.div(me, nz)
        self.z = lax.rem(me, nz)
        self.up = self.at(self.y, lax.rem(self.z + 1, nz))
        self.down = self.at(self.y, lax.rem(self.z + nz - 1, nz))
        order = sorted(range(1, ny), key=lambda j: -min(j, ny - j))
        self.across = [lax.rem(self.y + j, ny) for j in order]

    def at(self, y, z):
        return {"seq": y * self.nz + z}


def remote(src, dst, send_sem, recv_sem, device):
    return pltpu.make_async_remote_copy(
        src_ref=src,
        dst_ref=dst,
        send_sem=send_sem,
        recv_sem=recv_sem,
        device_id=device,
        device_id_type=MESH,
    )


MINOR = (((1,), (1,)), ((), ()))
MAJOR = (((0,), (0,)), ((), ()))


def iota(shape, dim):
    return lax.broadcasted_iota(jnp.int32, shape, dim)


def inverse_norm(values):
    return lax.rsqrt(jnp.mean(values * values, axis=-1, keepdims=True) + EPS)


def kernel(
    ny, nz, nb,
    q_hbm, do_hbm, states_ref, gain_ref, kv_hbm, owners_ref, slots_ref,
    dq_ref, out_ref, gain_out_ref,
    ring, tabs, tab, pos, outs, recv, acc, mine, grad_rows, keys_kept, scores_kept, ids, ids_before, weight,
    back_outs, back, sums_in, sums_out, added, own, by_x, by_core, by_y, by_z, q_ref, do_ref, kv_ref,
    ring_send, ring_recv, y_send, y_recv, tab_send, tab_recv, id_send, id_recv, w_send, w_recv,
    sum_send, sum_recv, back_send, back_recv, x_send, x_recv, core_send, core_recv, gy_send, gy_recv, z_send, z_recv,
    in_sems,
):
    half = nz // 2
    place = Place(ny, nz)
    y, z, b = place.y, place.z, lax.axis_index("batch")
    me = y * nz + z
    rows, width = states_ref.shape
    part = rows // CHUNKS
    wide = outs.shape[1]
    block = wide // ny
    wanted = acc.shape[0]
    pieces = 2 * CAP
    length = block // pieces
    steps_pad = tab.shape[0]
    count = ny * nz
    following = {"seq": lax.rem(me + 1, count)}
    preceding = {"seq": lax.rem(me + count - 1, count)}
    x_peers = [lax.rem(b + j * X_CORES, nb) for j in range(1, nb // X_CORES)]
    z_peers = [lax.rem(z + j, nz) for j in range(1, nz)]
    core = lax.rem(b, X_CORES)
    right = lax.rem(b + X_CORES, nb)
    left = lax.rem(b + nb - X_CORES, nb)
    opposite = lax.rem(b + 2 * X_CORES, nb)
    sibling = b + 1 - 2 * core


    def ring_part(slot, way, chunk):
        return ring.at[slot, pl.ds(way * rows + chunk * part, part)]

    def forward(slot, way, chunk):
        far = isinstance(slot, int) and slot == half - 1
        first = isinstance(slot, int) and slot == 0
        src = ring_part(half - 1, 0, chunk) if first else ring_part(slot - 1, way, chunk)
        dst = ring_part(slot, 1, chunk) if far else ring_part(slot, way, chunk)
        return remote(
            src,
            dst,
            ring_send,
            ring_recv.at[slot, way, chunk],
            place.down if way == 0 else place.up,
        )


    main, rest = MAIN * length, block - MAIN * length

    def exchange(out, into, send, arrived, slot, j):
        there = place.across[j]
        first, size, row = 0, block, slot
        if isinstance(slot, int) and slot == half - 1:
            size = main
        elif isinstance(slot, int) and slot == half:
            first, size, row = ny * main, rest, half - 1
        return remote(
            out.at[row, pl.ds(first + there * size, size)],
            into.at[row, pl.ds(first + y * size, size)],
            send,
            arrived.at[slot, j],
            place.at(there, z),
        )

    def keep(out, into, slot):
        if isinstance(slot, int) and slot == half - 1:
            here = pl.ds(y * main, main)
            into[half - 1, here] = out[half - 1, here]
        elif isinstance(slot, int) and slot == half:
            here = pl.ds(ny * main + y * rest, rest)
            into[half - 1, here] = out[half - 1, here]
        else:
            here = pl.ds(y * block, block)
            into[slot, here] = out[slot, here]

    def across(slot, j):
        return exchange(outs, recv, y_send, y_recv, slot, j)

    def return_across(slot, j):
        return exchange(back_outs, back, back_send, back_recv, slot, j)

    def table_copy(j):
        there = place.across[j]
        return remote(
            tabs.at[ny + there], tabs.at[y], tab_send, tab_recv, place.at(there, z)
        )


    depth = kv_hbm.shape[0]
    cut = (depth + 31) // 32 * 16
    weight_parts = ((0, cut), (cut, depth - cut))

    def weight_copy(channel, number):
        first, size = weight_parts[number]
        if channel == 2:
            shard, device = (left, right) if number == 0 else (right, left)
        else:
            shard = (b, b, None, b, left, right, opposite)[channel]
            device = (right, left, None, sibling, sibling, sibling, sibling)[channel]
        there = weight.at[pl.ds(pl.multiple_of(shard * depth + first, 16), size)]
        return remote(
            there,
            there,
            w_send,
            w_recv.at[channel, number],
            {"batch": device},
        )

    def weights_one():
        answer()
        for number in range(2):
            weight_copy(3, number).start()
        weight_copy(0, 0).wait_recv()
        weight_copy(2, 0).start()
        weight_copy(4, 0).start()
        weight_copy(1, 1).wait_recv()
        weight_copy(2, 1).start()
        weight_copy(5, 1).start()

    def weights_two():
        weight_copy(0, 1).wait_recv()
        weight_copy(4, 1).start()
        weight_copy(1, 0).wait_recv()
        weight_copy(5, 0).start()

    def weights_three():
        for number in range(2):
            weight_copy(2, number).wait_recv()
            weight_copy(6, number).start()


    def part_of(ref, slot, way, chunk):
        return ref.at[slot, pl.ds(way * rows + chunk * part, part)]

    def pass_on(distance, way, chunk):
        far = isinstance(distance, int) and distance == half
        return remote(
            part_of(sums_out, distance - 1, 1 if far else way, chunk),
            part_of(sums_in, distance - 1, way, chunk),
            sum_send,
            sum_recv.at[distance - 1, way, chunk],
            place.up if way == 0 else place.down,
        )

    def all_of(ref, send, arrived):
        return remote(ref, ref, send, arrived, place.up)


    x = lax.div(b, X_CORES)

    def x_copy(j):
        return remote(
            by_x.at[x], by_x.at[x], x_send, x_recv, {"batch": x_peers[j]}
        )

    def core_copy():
        return remote(
            by_core.at[core], by_core.at[core], core_send, core_recv, {"batch": sibling}
        )

    def gy_copy(j):
        return remote(
            by_y.at[y], by_y.at[y], gy_send, gy_recv, place.at(place.across[j], z)
        )

    def z_copy(j):
        return remote(
            by_z.at[z], by_z.at[z], z_send, z_recv, place.at(y, z_peers[j])
        )

    def total(ref):
        result = ref[0]
        for i in range(1, ref.shape[0]):
            result = result + ref[i]
        return result


    kv_in = pltpu.make_async_copy(kv_hbm, kv_ref, in_sems.at[0])
    q_in = pltpu.make_async_copy(q_hbm, q_ref, in_sems.at[1])
    do_in = pltpu.make_async_copy(do_hbm, do_ref, in_sems.at[2])
    for copy in (kv_in, q_in, do_in):
        copy.start()

    gain = gain_ref[...].reshape(1, width)
    values = states_ref[...].astype(F32)
    ring[half - 1, :rows] = (values * inverse_norm(values) * gain).astype(BF16)
    ids[...] = jnp.zeros_like(ids)
    group = owners_ref.shape[2]
    for i in range(owners_ref.shape[1]):
        ids[0:1, i * group : (i + 1) * group] = owners_ref[0, i : i + 1]
        ids[1:2, i * group : (i + 1) * group] = slots_ref[0, i : i + 1]

    barrier = pltpu.get_barrier_semaphore()

    def tell(device):
        pl.semaphore_signal(barrier, inc=1, device_id=device, device_id_type=MESH)

    peers = (
        [place.up, place.down, preceding]
        + [place.at(there, z) for there in place.across]
        + [{"batch": peer} for peer in x_peers]
    )
    for peer in peers:
        tell(peer)

    @pl.when(core == 0)
    def _():
        pl.semaphore_wait(barrier, len(peers))

    @pl.when(core == 1)
    def _():
        pl.semaphore_wait(barrier, len(peers) + 1)

    tell({"batch": sibling})

    def answer():
        @pl.when(core == 0)
        def _():
            pl.semaphore_wait(barrier, 1)

    ids_copy = remote(ids, ids_before, id_send, id_recv, following)
    ids_copy.start()
    for chunk in range(CHUNKS):
        for way in range(2):
            forward(0, way, chunk).start()


    own_count = 2 * group
    request_count = own_count + group
    ids_copy.wait()
    lane = iota(ids.shape, 1)
    merged = jnp.where(lane < own_count, ids[...], pltpu.roll(ids_before[...], group, 1))
    known = (lane < own_count) | ((lane < request_count) & (me > 0))
    owner = jnp.where(known, merged, -1)[0:1]
    slot_id = merged[1:2]
    lane = lane[0:1]
    rank = jnp.where(lane < own_count, 0, CAP - 1)
    wide_owner = jnp.broadcast_to(owner, ids.shape)
    for shift in range(1, 2 * group):
        other = pltpu.roll(wide_owner, shift, 1)[0:1]
        source = lane - shift
        same = (other == owner) & (source >= 0) & (source < group)
        rank = jnp.where(same & (lane >= group) & (lane < own_count), 1, rank)
    column = jnp.zeros_like(owner)
    for j in range(1, ny):
        column = column + jnp.where(owner >= j * nz, 1, 0)
    ahead = owner - column * nz - z
    ahead = jnp.where(ahead < 0, ahead + nz, ahead)
    way = jnp.where(ahead >= half, 1, 0)
    distance = jnp.where(ahead == 0, half, jnp.where(ahead > half, nz - ahead, ahead))
    piece = (1 - way) * CAP + rank
    cell = jnp.where(owner >= 0, column * steps_pad + distance - 1, -1)
    last = jnp.where(
        piece < MAIN, column * MAIN + piece, ny * MAIN + column * (pieces - MAIN) + piece - MAIN
    )
    number = jnp.where(distance == half, last, column * pieces + piece)
    number = jnp.where(owner >= 0, (distance - 1) * ny * pieces + number, -1)
    value = way * rows + slot_id * length + 1

    table_rows, table_lanes = ny * steps_pad, tab.shape[1]
    lanes_of = (table_lanes, lane.shape[1])
    cells = one_hot(iota((table_rows, lane.shape[1]), 0) == cell)

    def found_at(first, size, first_piece):
        row = iota(lanes_of, 0) - (first + y * size)
        inside = (row >= 0) & (row < size)
        return jnp.where(inside, lax.div(row, length) + first_piece, -1)

    def found_by(row_piece):
        chosen = jnp.where(row_piece == piece, value, 0).astype(F32).astype(BF16)
        return lax.dot_general(cells, chosen, MINOR, preferred_element_type=F32)

    whole = found_by(found_at(0, block, 0))
    cut_in_two = found_by(
        jnp.maximum(found_at(0, main, 0), found_at(ny * main, rest, MAIN))
    )
    step_of = lax.rem(iota((table_rows, table_lanes), 0), steps_pad)
    found = jnp.where(step_of == half - 1, cut_in_two, whole).astype(jnp.int32)
    token = lax.rem(iota((table_rows, table_lanes), 1), length)
    table = jnp.where(found > 0, found + token, 0)
    for j in range(ny):
        tabs[ny + j] = table[j * steps_pad : (j + 1) * steps_pad]
    for j in range(ny - 1):
        table_copy(j).start()
    tabs[pl.ds(y, 1)] = tabs[pl.ds(ny + y, 1)]

    spread_of = (pos.shape[1], lane.shape[1])
    spread = one_hot(lax.div(iota(spread_of, 0), length) == iota(spread_of, 1))
    numbers = jnp.broadcast_to(number, ids.shape).astype(F32).astype(BF16)
    placed = lax.dot_general(numbers, spread, MINOR, preferred_element_type=F32).astype(jnp.int32)
    token = lax.rem(iota(placed.shape, 1), length)
    pos[...] = jnp.where(placed >= 0, placed * length + token, -1)

    acc[...] = jnp.zeros_like(acc)
    kv_in.wait()
    own_shard = pl.ds(pl.multiple_of(b * depth, 16), depth)
    weight[own_shard, : kv_ref.shape[2]] = kv_ref[:, 0, :]
    weight[own_shard, kv_ref.shape[2] :] = kv_ref[:, 1, :]
    for number in range(2):
        weight_copy(0, number).start()
        weight_copy(1, 1 - number).start()


    def selected_in(rows_there, first, size):
        row = tab[half - 1 : half, first : first + size]
        return one_hot(iota((rows_there, size), 0) + 1 == row)

    def selected(slot):
        row = tab[pl.ds(slot, 1), :wide]
        return one_hot(iota((2 * rows, wide), 0) + 1 == row)

    def placing(slot):
        return one_hot(iota((wide, wanted), 0) + slot * wide == pos[0:1, :wanted])

    def pick_by(select, shards):
        return lax.dot_general(select, shards, MAJOR, preferred_element_type=F32).astype(BF16)

    def pick(slot):
        if isinstance(slot, int) and slot == half:
            outs[half - 1, ny * main :] = pick_by(
                selected_in(rows, ny * main, ny * rest), ring[half - 1, :rows]
            )
        elif isinstance(slot, int) and slot == half - 1:
            outs[half - 1, : ny * main] = pick_by(
                selected_in(2 * rows, 0, ny * main), ring[half - 1]
            )
        else:
            outs[slot] = pick_by(selected(slot), ring[slot])
        for j in range(ny - 1):
            across(slot, j).start()
        keep(outs, recv, slot)

    def take(slot):
        for j in range(ny - 1):
            across(slot, j).wait_recv()
            if isinstance(slot, int) and slot == half - 1:
                across(half, j).wait_recv()
        acc[...] += lax.dot_general(placing(slot), recv[slot], MAJOR, preferred_element_type=F32)

    def near(slot, last):
        hand_on(slot, last)
        pick(slot)

    def hand_on(slot, last):
        for chunk in range(CHUNKS):
            for way in range(2):
                forward(slot, way, chunk).wait_recv()
                if not last:
                    forward(slot + 1, way, chunk).start()
                elif way == chunk:
                    forward(half - 1, way, chunk).start()

    services = {2: weights_one, 4: weights_two}
    hand_on(0, half == 2)
    all_of(tabs.at[pl.ds(0, ny - 1)], tab_send, tab_recv).wait()
    asked = tabs[0]
    for j in range(1, ny):
        asked = asked + tabs[j]
    tab[...] = asked
    pick(half)
    pick(0)
    if half > 2:

        @pl.loop(1, half - 2)
        def _(slot):
            near(slot, False)
            take(slot - 1)
            for at, service in services.items():
                if at < half - 2:
                    pl.when(slot == at)(service)

        near(half - 2, True)
        take(half - 3)
    for at, service in services.items():
        if at >= half - 2:
            service()
    weights_three()
    for way in range(2):
        forward(half - 1, way, way).wait_recv()
    pick(half - 1)
    take(half - 2)
    for channel in range(3, 7):
        for number in range(2):
            weight_copy(channel, number).wait_recv()
    take(half - 1)
    mine[...] = acc[...].astype(BF16)


    q_in.wait()
    do_in.wait()
    tokens = q_ref.shape[0]
    scaling = 1.0 / math.sqrt(HEAD_DIM)
    turn = lax.div(iota((wanted, tokens), 1) + 1, GROUP)
    key_group = lax.div(iota((wanted, tokens), 0), GROUP)
    mask = lax.rem(turn + 2, 3) == key_group
    mask = mask & ((turn > 0) | (me > 0))
    pages = mine[...]
    heads_wide = min(8 * HEAD_DIM, q_ref.shape[1])
    steps = q_ref.shape[1] // heads_wide
    acc[...] = jnp.zeros_like(acc)

    @pl.loop(0, steps)
    def _(step):
        here = pl.ds(pl.multiple_of(step * heads_wide, heads_wide), heads_wide)
        there = pl.ds(
            pl.multiple_of((steps + step) * heads_wide, heads_wide), heads_wide
        )
        key_weight, value_weight = weight[:, here], weight[:, there]
        key_all = jnp.dot(pages, key_weight, preferred_element_type=F32).astype(BF16)
        value_all = jnp.dot(pages, value_weight, preferred_element_type=F32).astype(BF16)
        queries, grads = q_ref[:, here], do_ref[:, here]
        key_grads, value_grads = [], []
        keys_kept[:, here] = key_all
        for head in range(heads_wide // HEAD_DIM):
            columns = slice(head * HEAD_DIM, (head + 1) * HEAD_DIM)
            query, grad = queries[:, columns], grads[:, columns]
            key, val = key_all[:, columns], value_all[:, columns]
            scores = lax.dot_general(key, query, MINOR, preferred_element_type=F32) * scaling
            weights = jnp.where(mask, jnp.exp(scores), 0.0)
            over = jnp.sum(weights, axis=0, keepdims=True)
            probability = weights * (1.0 / jnp.where(over == 0.0, 1.0, over))
            grad_probability = lax.dot_general(val, grad, MINOR, preferred_element_type=F32)
            delta = jnp.sum(probability * grad_probability, axis=0, keepdims=True)
            grad_scores = (probability * (grad_probability - delta) * scaling).astype(BF16)
            low = probability.astype(BF16)
            scores_kept[:, pl.ds(here.start + head * HEAD_DIM, HEAD_DIM)] = grad_scores
            key_grads.append(jnp.dot(grad_scores, query, preferred_element_type=F32))
            value_grads.append(jnp.dot(low, grad, preferred_element_type=F32))
        key_grad = jnp.concatenate(key_grads, axis=1).astype(BF16)
        value_grad = jnp.concatenate(value_grads, axis=1).astype(BF16)
        change = lax.dot_general(key_grad, key_weight, MINOR, preferred_element_type=F32)
        change += lax.dot_general(value_grad, value_weight, MINOR, preferred_element_type=F32)
        acc[...] += change

    grad_rows[...] = acc[...].astype(BF16)

    def query_grad(head):
        here = pl.ds(pl.multiple_of(head * HEAD_DIM, HEAD_DIM), HEAD_DIM)
        dq_ref[:, here] = lax.dot_general(
            scores_kept[:, here], keys_kept[:, here], MAJOR, preferred_element_type=F32
        ).astype(BF16)


    def scatter(slot):
        back_outs[slot] = jnp.dot(placing(slot), grad_rows[...], preferred_element_type=F32).astype(BF16)
        for j in range(ny - 1):
            return_across(slot, j).start()
        keep(back_outs, back, slot)

    def scatter_rest():
        for j in range(ny - 1):
            return_across(half, j).start()
        keep(back_outs, back, half)

    def gather_by(select, blocks):
        return jnp.dot(select, blocks, preferred_element_type=F32)

    def gather(slot):
        for j in range(ny - 1):
            return_across(slot, j).wait_recv()
        added[...] = gather_by(selected(slot), back[slot])

    def gather_far():
        for j in range(ny - 1):
            return_across(half - 1, j).wait_recv()
        added[...] = gather_by(
            selected_in(2 * rows, 0, ny * main), back[half - 1, : ny * main]
        )

    def gather_rest():
        for j in range(ny - 1):
            return_across(half, j).wait_recv()
        own[...] += gather_by(
            selected_in(rows, ny * main, ny * rest), back[half - 1, ny * main :]
        )

    def relay(distance, first):
        gather(distance - 1)
        for chunk in range(CHUNKS):
            for way in range(2):
                here = pl.ds(way * rows + chunk * part, part)
                total_here = added[here]
                if not first or way == chunk:
                    pass_on(distance + 1, way, chunk).wait_recv()
                    total_here = total_here + sums_in[distance, here].astype(F32)
                sums_out[distance - 1, here] = total_here.astype(BF16)
                pass_on(distance, way, chunk).start()

    def pass_sent(ref, send):
        every = ref.at[pl.ds(0, half - 1)]
        all_of(every, send, send).wait_send()
        last = ref.at[half - 1, pl.ds(0, rows)]
        all_of(last, send, send).wait_send()

    def across_sent(ref, send):
        every = ref.at[:, pl.ds(0, wide - block)]
        all_of(every, send, send).wait_send()

    def fetch_sent():
        pass_sent(ring, ring_send)
        across_sent(outs, y_send)
        all_of(weight.at[pl.ds(0, 7 * depth)], w_send, w_send).wait_send()

    def gain_one():
        lanes = width // 128
        products = jnp.sum(grad_rows[...].astype(F32) * mine[...].astype(F32), axis=0, keepdims=True)
        products = products / gain
        by_x[pl.ds(x, 1)] = jnp.zeros_like(by_x[pl.ds(x, 1)])
        for i in range(lanes):
            by_x[x, i : i + 1] = products[:, i * 128 : (i + 1) * 128]
        for j in range(len(x_peers)):
            x_copy(j).start()

    def gain_two():
        all_of(by_x.at[pl.ds(0, len(x_peers))], x_send, x_recv).wait()
        by_core[core] = total(by_x)
        core_copy().start()

    def gain_three():
        core_copy().wait()
        by_y[y] = total(by_core)
        for j in range(ny - 1):
            gy_copy(j).start()

    def gain_four():
        all_of(by_y.at[pl.ds(0, ny - 1)], gy_send, gy_recv).wait()
        by_z[z] = total(by_y)
        for j in range(nz - 1):
            z_copy(j).start()

    scatter(half - 1)
    scatter(half - 2)
    scatter_rest()
    gain_one()
    fetch_sent()
    if half > 2:
        scatter(half - 3)
    gather_far()
    sums_out[half - 1, pl.ds(rows, rows)] = added[pl.ds(rows, rows)].astype(BF16)
    for way in range(2):
        pass_on(half, way, way).start()
    own[...] = added[:rows]
    gather_rest()
    relay(half - 1, True)
    gain_two()
    heads = q_ref.shape[1] // HEAD_DIM
    turns = max(half - 3, 0)
    each = heads // turns if turns else 0
    for head in range(each * turns, heads):
        query_grad(head)
    if half > 2:

        @pl.loop(0, half - 3)
        def _(i):
            distance = half - 2 - i
            scatter(distance - 2)
            relay(distance, False)
            pl.when(i == max(0, half - 6))(gain_three)
            for head in range(each):
                query_grad(i * each + head)

    else:
        gain_three()
    gain_four()
    if half > 2:
        relay(1, False)

    all_of(by_z.at[pl.ds(0, nz - 1)], z_send, z_recv).wait()
    result = total(by_z)
    for i in range(width // 128):
        gain_out_ref[i * 128 : (i + 1) * 128] = result[i]

    for chunk in range(CHUNKS):
        here = pl.ds(chunk * part, part)
        for way in range(2):
            pass_on(1, way, chunk).wait_recv()
        normed_grad = own[here] + sums_in[0, here].astype(F32)
        normed_grad = normed_grad + sums_in[0, pl.ds(rows + chunk * part, part)].astype(F32)
        values = states_ref[here].astype(F32)
        inverse = inverse_norm(values)
        scaled = normed_grad * gain
        inner = jnp.mean(scaled * values, axis=-1, keepdims=True)
        out_ref[here] = (
            inverse * scaled - values * (inverse * inverse * inverse * inner)
        ).astype(BF16)

    pass_sent(sums_out, sum_send)
    across_sent(back_outs, back_send)


def on_device(ny, nz, nb, queries, out_grad, states, gain, kv_weight, owners, slots):
    held, length, enc = states.shape[1:]
    tokens, width = queries.shape[1:]
    half, rows = nz // 2, held * length
    wanted = owners.shape[1] * owners.shape[2] * 3 // 2 * length
    wide = ny * 2 * CAP * length
    table = (max(8, half), wide + -wide % 128)
    dma = pltpu.SemaphoreType.DMA
    query_grad, state_grad, gain_grad = pl.pallas_call(
        functools.partial(kernel, ny, nz, nb),
        out_shape=(
            jax.ShapeDtypeStruct((tokens, width), BF16),
            jax.ShapeDtypeStruct((rows, enc), BF16),
            jax.ShapeDtypeStruct((enc,), F32),
        ),
        in_specs=[
            pl.BlockSpec(memory_space=VMEM if inside else pl.ANY)
            for inside in (False, False, True, True, False, True, True)
        ],
        out_specs=(pl.BlockSpec(memory_space=VMEM),) * 3,
        scratch_shapes=[
            VMEM((half, 2 * rows, enc), BF16),
            VMEM((2 * ny,) + table, jnp.int32),
            VMEM(table, jnp.int32),
            VMEM((8, wanted + -wanted % 128), jnp.int32),
            VMEM((half, wide, enc), BF16),
            VMEM((half, wide, enc), BF16),
            VMEM((wanted, enc), F32),
            VMEM((wanted, enc), BF16),
            VMEM((wanted, enc), BF16),
            VMEM((wanted, width), BF16),
            VMEM((wanted, width), BF16),
            VMEM((8, 128), jnp.int32),
            VMEM((8, 128), jnp.int32),
            VMEM((enc, 2 * width), BF16),
            VMEM((half, wide, enc), BF16),
            VMEM((half, wide, enc), BF16),
            VMEM((half, 2 * rows, enc), BF16),
            VMEM((half, 2 * rows, enc), BF16),
            VMEM((2 * rows, enc), F32),
            VMEM((rows, enc), F32),
            VMEM((nb // X_CORES, 8, 128), F32),
            VMEM((X_CORES, 8, 128), F32),
            VMEM((ny, 8, 128), F32),
            VMEM((nz, 8, 128), F32),
            VMEM((tokens, width), BF16),
            VMEM((tokens, width), BF16),
            VMEM(kv_weight.shape, BF16),
            dma, dma((half, 2, CHUNKS)),
            dma, dma((half + 1, ny - 1)),
            dma, dma,
            dma, dma,
            dma, dma((7, 2)),
            dma, dma((half, 2, CHUNKS)),
            dma, dma((half + 1, ny - 1)),
            dma, dma,
            dma, dma,
            dma, dma,
            dma, dma,
            dma((3,)),
        ],
        compiler_params=pltpu.CompilerParams(
            collective_id=1, has_side_effects=True, vmem_limit_bytes=54 << 20
        ),
    )(
        queries[0], out_grad[0], states.reshape(rows, enc), gain, kv_weight, owners, slots,
    )
    return (
        query_grad[None],
        state_grad.reshape(1, held, length, enc),
        gain_grad,
    )


def solution(mesh):
    ny = Y_SIZE
    nz = mesh.shape["seq"] // ny
    nb = mesh.shape["batch"]
    return jax.shard_map(
        functools.partial(on_device, ny, nz, nb),
        mesh=mesh,
        in_specs=(
            P("batch", "seq", None),
            P("batch", "seq", None),
            P("batch", "seq", None, None),
            P(),
            P("batch", None, None),
            P("batch", "seq", None),
            P("batch", "seq", None),
        ),
        out_specs=(P("batch", "seq", None), P("batch", "seq", None, None), P()),
        check_vma=False,
    )
```

```python
import functools
import math

import jax
import jax.numpy as jnp
from jax import lax
from jax.experimental import pallas as pl
from jax.experimental.pallas import tpu as pltpu
from jax.sharding import PartitionSpec as P

HEAD_DIM = 128
GROUP = 64
EPS = 1e-06
Y_SIZE = 4
CHUNKS = 2
FETCH_ORDER = ((0, 0), (1, 1), (0, 1), (1, 0))
RETURN_ORDER = ((0, 1), (1, 0), (0, 0), (1, 1))
X_CORES = 2
MAIN = 4
CAP = 3

MESH = pl.DeviceIdType.MESH
VMEM = pltpu.VMEM
F32 = jnp.float32
BF16 = jnp.bfloat16


def one_hot(mask):
    return jnp.where(mask, 1.0, 0.0).astype(BF16)


class Place:
    def __init__(self, ny, nz):
        me = lax.axis_index("seq")
        self.ny, self.nz = ny, nz
        self.y = lax.div(me, nz)
        self.z = lax.rem(me, nz)
        self.up = self.at(self.y, lax.rem(self.z + 1, nz))
        self.down = self.at(self.y, lax.rem(self.z + nz - 1, nz))
        order = sorted(range(1, ny), key=lambda j: -min(j, ny - j))
        self.across = [lax.rem(self.y + j, ny) for j in order]

    def at(self, y, z):
        return {"seq": y * self.nz + z}


def remote(src, dst, send_sem, recv_sem, device):
    return pltpu.make_async_remote_copy(
        src_ref=src,
        dst_ref=dst,
        send_sem=send_sem,
        recv_sem=recv_sem,
        device_id=device,
        device_id_type=MESH,
    )


MINOR = (((1,), (1,)), ((), ()))
MAJOR = (((0,), (0,)), ((), ()))


def iota(shape, dim):
    return lax.broadcasted_iota(jnp.int32, shape, dim)


def inverse_norm(values):
    return lax.rsqrt(jnp.mean(values * values, axis=-1, keepdims=True) + EPS)


def kernel(
    ny, nz, nb,
    q_hbm, do_hbm, states_ref, gain_ref, kv_hbm, owners_ref, slots_ref,
    dq_ref, out_ref, gain_out_ref,
    ring, tabs, tab, pos, outs, recv, acc, mine, grad_rows, keys_kept, scores_kept, ids, ids_before, weight,
    back_outs, back, sums_in, sums_out, added, own, by_x, by_core, by_y, by_z, q_ref, do_ref, kv_ref,
    ring_send, ring_recv, y_send, y_recv, tab_send, tab_recv, id_send, id_recv, w_send, w_recv,
    sum_send, sum_recv, back_send, back_recv, x_send, x_recv, core_send, core_recv, gy_send, gy_recv, z_send, z_recv,
    in_sems,
):
    half = nz // 2
    place = Place(ny, nz)
    y, z, b = place.y, place.z, lax.axis_index("batch")
    me = y * nz + z
    rows, width = states_ref.shape
    part = rows // CHUNKS
    wide = outs.shape[1]
    block = wide // ny
    wanted = acc.shape[0]
    pieces = 2 * CAP
    length = block // pieces
    steps_pad = tab.shape[0]
    count = ny * nz
    following = {"seq": lax.rem(me + 1, count)}
    preceding = {"seq": lax.rem(me + count - 1, count)}
    x_peers = [lax.rem(b + j * X_CORES, nb) for j in range(1, nb // X_CORES)]
    z_peers = [lax.rem(z + j, nz) for j in range(1, nz)]
    core = lax.rem(b, X_CORES)
    right = lax.rem(b + X_CORES, nb)
    left = lax.rem(b + nb - X_CORES, nb)
    opposite = lax.rem(b + 2 * X_CORES, nb)
    sibling = b + 1 - 2 * core


    def ring_part(slot, way, chunk):
        return ring.at[slot, pl.ds(way * rows + chunk * part, part)]

    def forward(slot, way, chunk):
        far = isinstance(slot, int) and slot == half - 1
        first = isinstance(slot, int) and slot == 0
        src = ring_part(half - 1, 0, chunk) if first else ring_part(slot - 1, way, chunk)
        dst = ring_part(slot, 1, chunk) if far else ring_part(slot, way, chunk)
        return remote(
            src,
            dst,
            ring_send,
            ring_recv.at[slot, way, chunk],
            place.down if way == 0 else place.up,
        )


    main, rest = MAIN * length, block - MAIN * length

    def exchange(out, into, send, arrived, slot, j):
        there = place.across[j]
        first, size, row = 0, block, slot
        if isinstance(slot, int) and slot == half - 1:
            size = main
        elif isinstance(slot, int) and slot == half:
            first, size, row = ny * main, rest, half - 1
        return remote(
            out.at[row, pl.ds(first + there * size, size)],
            into.at[row, pl.ds(first + y * size, size)],
            send,
            arrived.at[slot, j],
            place.at(there, z),
        )

    def keep(out, into, slot):
        if isinstance(slot, int) and slot == half - 1:
            here = pl.ds(y * main, main)
            into[half - 1, here] = out[half - 1, here]
        elif isinstance(slot, int) and slot == half:
            here = pl.ds(ny * main + y * rest, rest)
            into[half - 1, here] = out[half - 1, here]
        else:
            here = pl.ds(y * block, block)
            into[slot, here] = out[slot, here]

    def across(slot, j):
        return exchange(outs, recv, y_send, y_recv, slot, j)

    def return_across(slot, j):
        return exchange(back_outs, back, back_send, back_recv, slot, j)

    def table_copy(j):
        there = place.across[j]
        return remote(
            tabs.at[ny + there], tabs.at[y], tab_send, tab_recv, place.at(there, z)
        )


    depth = kv_hbm.shape[0]
    cut = (depth + 31) // 32 * 16
    weight_parts = ((0, cut), (cut, depth - cut))

    def weight_copy(channel, number):
        first, size = weight_parts[number]
        if channel == 2:
            shard, device = (left, right) if number == 0 else (right, left)
        else:
            shard = (b, b, None, b, left, right, opposite)[channel]
            device = (right, left, None, sibling, sibling, sibling, sibling)[channel]
        there = weight.at[pl.ds(pl.multiple_of(shard * depth + first, 16), size)]
        return remote(
            there,
            there,
            w_send,
            w_recv.at[channel, number],
            {"batch": device},
        )

    def weights_one():
        answer()
        for number in range(2):
            weight_copy(3, number).start()
        weight_copy(0, 0).wait_recv()
        weight_copy(2, 0).start()
        weight_copy(4, 0).start()
        weight_copy(1, 1).wait_recv()
        weight_copy(2, 1).start()
        weight_copy(5, 1).start()

    def weights_two():
        weight_copy(0, 1).wait_recv()
        weight_copy(4, 1).start()
        weight_copy(1, 0).wait_recv()
        weight_copy(5, 0).start()

    def weights_three():
        for number in range(2):
            weight_copy(2, number).wait_recv()
            weight_copy(6, number).start()


    def part_of(ref, slot, way, chunk):
        return ref.at[slot, pl.ds(way * rows + chunk * part, part)]

    def pass_on(distance, way, chunk):
        far = isinstance(distance, int) and distance == half
        return remote(
            part_of(sums_out, distance - 1, 1 if far else way, chunk),
            part_of(sums_in, distance - 1, way, chunk),
            sum_send,
            sum_recv.at[distance - 1, way, chunk],
            place.up if way == 0 else place.down,
        )

    def all_of(ref, send, arrived):
        return remote(ref, ref, send, arrived, place.up)


    x = lax.div(b, X_CORES)

    def x_copy(j):
        return remote(
            by_x.at[x], by_x.at[x], x_send, x_recv, {"batch": x_peers[j]}
        )

    def core_copy():
        return remote(
            by_core.at[core], by_core.at[core], core_send, core_recv, {"batch": sibling}
        )

    def gy_copy(j):
        return remote(
            by_y.at[y], by_y.at[y], gy_send, gy_recv, place.at(place.across[j], z)
        )

    def z_copy(j):
        return remote(
            by_z.at[z], by_z.at[z], z_send, z_recv, place.at(y, z_peers[j])
        )

    def total(ref):
        result = ref[0]
        for i in range(1, ref.shape[0]):
            result = result + ref[i]
        return result


    kv_in = pltpu.make_async_copy(kv_hbm, kv_ref, in_sems.at[0])
    q_in = pltpu.make_async_copy(q_hbm, q_ref, in_sems.at[1])
    do_in = pltpu.make_async_copy(do_hbm, do_ref, in_sems.at[2])
    for copy in (kv_in, q_in, do_in):
        copy.start()

    gain = gain_ref[...].reshape(1, width)
    values = states_ref[...].astype(F32)
    ring[half - 1, :rows] = (values * inverse_norm(values) * gain).astype(BF16)
    ids[...] = jnp.zeros_like(ids)
    group = owners_ref.shape[2]
    for i in range(owners_ref.shape[1]):
        ids[0:1, i * group : (i + 1) * group] = owners_ref[0, i : i + 1]
        ids[1:2, i * group : (i + 1) * group] = slots_ref[0, i : i + 1]

    barrier = pltpu.get_barrier_semaphore()

    def tell(device):
        pl.semaphore_signal(barrier, inc=1, device_id=device, device_id_type=MESH)

    peers = (
        [place.up, place.down, preceding]
        + [place.at(there, z) for there in place.across]
        + [{"batch": peer} for peer in x_peers]
    )
    for peer in peers:
        tell(peer)

    @pl.when(core == 0)
    def _():
        pl.semaphore_wait(barrier, len(peers))

    @pl.when(core == 1)
    def _():
        pl.semaphore_wait(barrier, len(peers) + 1)

    tell({"batch": sibling})

    def answer():
        @pl.when(core == 0)
        def _():
            pl.semaphore_wait(barrier, 1)

    ids_copy = remote(ids, ids_before, id_send, id_recv, following)
    ids_copy.start()
    for way, chunk in FETCH_ORDER:
        forward(0, way, chunk).start()


    own_count = 2 * group
    request_count = own_count + group
    ids_copy.wait()
    lane = iota(ids.shape, 1)
    merged = jnp.where(lane < own_count, ids[...], pltpu.roll(ids_before[...], group, 1))
    known = (lane < own_count) | ((lane < request_count) & (me > 0))
    owner = jnp.where(known, merged, -1)[0:1]
    slot_id = merged[1:2]
    lane = lane[0:1]
    rank = jnp.where(lane < own_count, 0, CAP - 1)
    wide_owner = jnp.broadcast_to(owner, ids.shape)
    for shift in range(1, 2 * group):
        other = pltpu.roll(wide_owner, shift, 1)[0:1]
        source = lane - shift
        same = (other == owner) & (source >= 0) & (source < group)
        rank = jnp.where(same & (lane >= group) & (lane < own_count), 1, rank)
    column = jnp.zeros_like(owner)
    for j in range(1, ny):
        column = column + jnp.where(owner >= j * nz, 1, 0)
    ahead = owner - column * nz - z
    ahead = jnp.where(ahead < 0, ahead + nz, ahead)
    way = jnp.where(ahead >= half, 1, 0)
    distance = jnp.where(ahead == 0, half, jnp.where(ahead > half, nz - ahead, ahead))
    piece = (1 - way) * CAP + rank
    cell = jnp.where(owner >= 0, column * steps_pad + distance - 1, -1)
    last = jnp.where(
        piece < MAIN, column * MAIN + piece, ny * MAIN + column * (pieces - MAIN) + piece - MAIN
    )
    number = jnp.where(distance == half, last, column * pieces + piece)
    number = jnp.where(owner >= 0, (distance - 1) * ny * pieces + number, -1)
    value = way * rows + slot_id * length + 1

    table_rows, table_lanes = ny * steps_pad, tab.shape[1]
    lanes_of = (table_lanes, lane.shape[1])
    cells = one_hot(iota((table_rows, lane.shape[1]), 0) == cell)

    def found_at(first, size, first_piece):
        row = iota(lanes_of, 0) - (first + y * size)
        inside = (row >= 0) & (row < size)
        return jnp.where(inside, lax.div(row, length) + first_piece, -1)

    def found_by(row_piece):
        chosen = jnp.where(row_piece == piece, value, 0).astype(F32).astype(BF16)
        return lax.dot_general(cells, chosen, MINOR, preferred_element_type=F32)

    whole = found_by(found_at(0, block, 0))
    cut_in_two = found_by(
        jnp.maximum(found_at(0, main, 0), found_at(ny * main, rest, MAIN))
    )
    step_of = lax.rem(iota((table_rows, table_lanes), 0), steps_pad)
    found = jnp.where(step_of == half - 1, cut_in_two, whole).astype(jnp.int32)
    token = lax.rem(iota((table_rows, table_lanes), 1), length)
    table = jnp.where(found > 0, found + token, 0)
    for j in range(ny):
        tabs[ny + j] = table[j * steps_pad : (j + 1) * steps_pad]
    for j in range(ny - 1):
        table_copy(j).start()
    tabs[pl.ds(y, 1)] = tabs[pl.ds(ny + y, 1)]

    spread_of = (pos.shape[1], lane.shape[1])
    spread = one_hot(lax.div(iota(spread_of, 0), length) == iota(spread_of, 1))
    numbers = jnp.broadcast_to(number, ids.shape).astype(F32).astype(BF16)
    placed = lax.dot_general(numbers, spread, MINOR, preferred_element_type=F32).astype(jnp.int32)
    token = lax.rem(iota(placed.shape, 1), length)
    pos[...] = jnp.where(placed >= 0, placed * length + token, -1)

    acc[...] = jnp.zeros_like(acc)
    kv_in.wait()
    own_shard = pl.ds(pl.multiple_of(b * depth, 16), depth)
    weight[own_shard, : kv_ref.shape[2]] = kv_ref[:, 0, :]
    weight[own_shard, kv_ref.shape[2] :] = kv_ref[:, 1, :]
    for number in range(2):
        weight_copy(0, number).start()
        weight_copy(1, 1 - number).start()


    def selected_in(rows_there, first, size):
        row = tab[half - 1 : half, first : first + size]
        return one_hot(iota((rows_there, size), 0) + 1 == row)

    def selected(slot):
        row = tab[pl.ds(slot, 1), :wide]
        return one_hot(iota((2 * rows, wide), 0) + 1 == row)

    def placing(slot):
        return one_hot(iota((wide, wanted), 0) + slot * wide == pos[0:1, :wanted])

    def pick_by(select, shards):
        return lax.dot_general(select, shards, MAJOR, preferred_element_type=F32).astype(BF16)

    def pick(slot):
        if isinstance(slot, int) and slot == half:
            outs[half - 1, ny * main :] = pick_by(
                selected_in(rows, ny * main, ny * rest), ring[half - 1, :rows]
            )
        elif isinstance(slot, int) and slot == half - 1:
            outs[half - 1, : ny * main] = pick_by(
                selected_in(2 * rows, 0, ny * main), ring[half - 1]
            )
        else:
            outs[slot] = pick_by(selected(slot), ring[slot])
        for j in range(ny - 1):
            across(slot, j).start()
        keep(outs, recv, slot)

    def take(slot):
        for j in range(ny - 1):
            across(slot, j).wait_recv()
            if isinstance(slot, int) and slot == half - 1:
                across(half, j).wait_recv()
        acc[...] += lax.dot_general(placing(slot), recv[slot], MAJOR, preferred_element_type=F32)

    def near(slot, last):
        hand_on(slot, last)
        pick(slot)

    def hand_on(slot, last):
        for way, chunk in FETCH_ORDER:
            forward(slot, way, chunk).wait_recv()
            if not last:
                forward(slot + 1, way, chunk).start()
            elif way == chunk:
                forward(half - 1, way, chunk).start()

    services = {2: weights_one, 4: weights_two}
    hand_on(0, half == 2)
    all_of(tabs.at[pl.ds(0, ny - 1)], tab_send, tab_recv).wait()
    asked = tabs[0]
    for j in range(1, ny):
        asked = asked + tabs[j]
    tab[...] = asked
    pick(half)
    pick(0)
    if half > 2:

        @pl.loop(1, half - 2)
        def _(slot):
            near(slot, False)
            take(slot - 1)
            for at, service in services.items():
                if at < half - 2:
                    pl.when(slot == at)(service)

        near(half - 2, True)
        take(half - 3)
    for at, service in services.items():
        if at >= half - 2:
            service()
    weights_three()
    for way in range(2):
        forward(half - 1, way, way).wait_recv()
    pick(half - 1)
    take(half - 2)
    for channel in range(3, 7):
        for number in range(2):
            weight_copy(channel, number).wait_recv()
    take(half - 1)
    mine[...] = acc[...].astype(BF16)


    q_in.wait()
    do_in.wait()
    tokens = q_ref.shape[0]
    scaling = 1.0 / math.sqrt(HEAD_DIM)
    turn = lax.div(iota((wanted, tokens), 1) + 1, GROUP)
    key_group = lax.div(iota((wanted, tokens), 0), GROUP)
    mask = lax.rem(turn + 2, 3) == key_group
    mask = mask & ((turn > 0) | (me > 0))
    pages = mine[...]
    heads_wide = min(8 * HEAD_DIM, q_ref.shape[1])
    steps = q_ref.shape[1] // heads_wide
    acc[...] = jnp.zeros_like(acc)

    @pl.loop(0, steps)
    def _(step):
        here = pl.ds(pl.multiple_of(step * heads_wide, heads_wide), heads_wide)
        there = pl.ds(
            pl.multiple_of((steps + step) * heads_wide, heads_wide), heads_wide
        )
        key_weight, value_weight = weight[:, here], weight[:, there]
        key_all = jnp.dot(pages, key_weight, preferred_element_type=F32).astype(BF16)
        value_all = jnp.dot(pages, value_weight, preferred_element_type=F32).astype(BF16)
        queries, grads = q_ref[:, here], do_ref[:, here]
        key_grads, value_grads = [], []
        keys_kept[:, here] = key_all
        for head in range(heads_wide // HEAD_DIM):
            columns = slice(head * HEAD_DIM, (head + 1) * HEAD_DIM)
            query, grad = queries[:, columns], grads[:, columns]
            key, val = key_all[:, columns], value_all[:, columns]
            scores = lax.dot_general(key, query, MINOR, preferred_element_type=F32) * scaling
            weights = jnp.where(mask, jnp.exp(scores), 0.0)
            over = jnp.sum(weights, axis=0, keepdims=True)
            probability = weights * (1.0 / jnp.where(over == 0.0, 1.0, over))
            grad_probability = lax.dot_general(val, grad, MINOR, preferred_element_type=F32)
            delta = jnp.sum(probability * grad_probability, axis=0, keepdims=True)
            grad_scores = (probability * (grad_probability - delta) * scaling).astype(BF16)
            low = probability.astype(BF16)
            scores_kept[:, pl.ds(here.start + head * HEAD_DIM, HEAD_DIM)] = grad_scores
            key_grads.append(jnp.dot(grad_scores, query, preferred_element_type=F32))
            value_grads.append(jnp.dot(low, grad, preferred_element_type=F32))
        key_grad = jnp.concatenate(key_grads, axis=1).astype(BF16)
        value_grad = jnp.concatenate(value_grads, axis=1).astype(BF16)
        change = lax.dot_general(key_grad, key_weight, MINOR, preferred_element_type=F32)
        change += lax.dot_general(value_grad, value_weight, MINOR, preferred_element_type=F32)
        acc[...] += change

    grad_rows[...] = acc[...].astype(BF16)

    def query_grad(head):
        here = pl.ds(pl.multiple_of(head * HEAD_DIM, HEAD_DIM), HEAD_DIM)
        dq_ref[:, here] = lax.dot_general(
            scores_kept[:, here], keys_kept[:, here], MAJOR, preferred_element_type=F32
        ).astype(BF16)


    def scatter(slot):
        back_outs[slot] = jnp.dot(placing(slot), grad_rows[...], preferred_element_type=F32).astype(BF16)
        for j in range(ny - 1):
            return_across(slot, j).start()
        keep(back_outs, back, slot)

    def scatter_rest():
        for j in range(ny - 1):
            return_across(half, j).start()
        keep(back_outs, back, half)

    def gather_by(select, blocks):
        return jnp.dot(select, blocks, preferred_element_type=F32)

    def gather(slot):
        for j in range(ny - 1):
            return_across(slot, j).wait_recv()
        added[...] = gather_by(selected(slot), back[slot])

    def gather_far():
        for j in range(ny - 1):
            return_across(half - 1, j).wait_recv()
        added[...] = gather_by(
            selected_in(2 * rows, 0, ny * main), back[half - 1, : ny * main]
        )

    def gather_rest():
        for j in range(ny - 1):
            return_across(half, j).wait_recv()
        own[...] += gather_by(
            selected_in(rows, ny * main, ny * rest), back[half - 1, ny * main :]
        )

    def relay(distance, first):
        gather(distance - 1)
        for way, chunk in RETURN_ORDER:
            here = pl.ds(way * rows + chunk * part, part)
            total_here = added[here]
            if not first or way == chunk:
                pass_on(distance + 1, way, chunk).wait_recv()
                total_here = total_here + sums_in[distance, here].astype(F32)
            sums_out[distance - 1, here] = total_here.astype(BF16)
            pass_on(distance, way, chunk).start()

    def pass_sent(ref, send):
        every = ref.at[pl.ds(0, half - 1)]
        all_of(every, send, send).wait_send()
        last = ref.at[half - 1, pl.ds(0, rows)]
        all_of(last, send, send).wait_send()

    def across_sent(ref, send):
        every = ref.at[:, pl.ds(0, wide - block)]
        all_of(every, send, send).wait_send()

    def fetch_sent():
        pass_sent(ring, ring_send)
        across_sent(outs, y_send)
        all_of(weight.at[pl.ds(0, 7 * depth)], w_send, w_send).wait_send()

    def gain_one():
        lanes = width // 128
        products = jnp.sum(grad_rows[...].astype(F32) * mine[...].astype(F32), axis=0, keepdims=True)
        products = products / gain
        by_x[pl.ds(x, 1)] = jnp.zeros_like(by_x[pl.ds(x, 1)])
        for i in range(lanes):
            by_x[x, i : i + 1] = products[:, i * 128 : (i + 1) * 128]
        for j in range(len(x_peers)):
            x_copy(j).start()

    def gain_two():
        all_of(by_x.at[pl.ds(0, len(x_peers))], x_send, x_recv).wait()
        by_core[core] = total(by_x)
        core_copy().start()

    def gain_three():
        core_copy().wait()
        by_y[y] = total(by_core)
        for j in range(ny - 1):
            gy_copy(j).start()

    def gain_four():
        all_of(by_y.at[pl.ds(0, ny - 1)], gy_send, gy_recv).wait()
        by_z[z] = total(by_y)
        for j in range(nz - 1):
            z_copy(j).start()

    scatter(half - 1)
    scatter(half - 2)
    scatter_rest()
    gain_one()
    fetch_sent()
    if half > 2:
        scatter(half - 3)
    gather_far()
    sums_out[half - 1, pl.ds(rows, rows)] = added[pl.ds(rows, rows)].astype(BF16)
    for way in range(2):
        pass_on(half, way, way).start()
    own[...] = added[:rows]
    gather_rest()
    relay(half - 1, True)
    gain_two()
    heads = q_ref.shape[1] // HEAD_DIM
    turns = max(half - 3, 0)
    each = heads // turns if turns else 0
    for head in range(each * turns, heads):
        query_grad(head)
    if half > 2:

        @pl.loop(0, half - 3)
        def _(i):
            distance = half - 2 - i
            scatter(distance - 2)
            relay(distance, False)
            pl.when(i == max(0, half - 6))(gain_three)
            for head in range(each):
                query_grad(i * each + head)

    else:
        gain_three()
    gain_four()
    if half > 2:
        relay(1, False)

    all_of(by_z.at[pl.ds(0, nz - 1)], z_send, z_recv).wait()
    result = total(by_z)
    for i in range(width // 128):
        gain_out_ref[i * 128 : (i + 1) * 128] = result[i]

    for chunk in range(CHUNKS):
        here = pl.ds(chunk * part, part)
        for way in range(2):
            pass_on(1, way, chunk).wait_recv()
        normed_grad = own[here] + sums_in[0, here].astype(F32)
        normed_grad = normed_grad + sums_in[0, pl.ds(rows + chunk * part, part)].astype(F32)
        values = states_ref[here].astype(F32)
        inverse = inverse_norm(values)
        scaled = normed_grad * gain
        inner = jnp.mean(scaled * values, axis=-1, keepdims=True)
        out_ref[here] = (
            inverse * scaled - values * (inverse * inverse * inverse * inner)
        ).astype(BF16)

    pass_sent(sums_out, sum_send)
    across_sent(back_outs, back_send)


def on_device(ny, nz, nb, queries, out_grad, states, gain, kv_weight, owners, slots):
    held, length, enc = states.shape[1:]
    tokens, width = queries.shape[1:]
    half, rows = nz // 2, held * length
    wanted = owners.shape[1] * owners.shape[2] * 3 // 2 * length
    wide = ny * 2 * CAP * length
    table = (max(8, half), wide + -wide % 128)
    dma = pltpu.SemaphoreType.DMA
    query_grad, state_grad, gain_grad = pl.pallas_call(
        functools.partial(kernel, ny, nz, nb),
        out_shape=(
            jax.ShapeDtypeStruct((tokens, width), BF16),
            jax.ShapeDtypeStruct((rows, enc), BF16),
            jax.ShapeDtypeStruct((enc,), F32),
        ),
        in_specs=[
            pl.BlockSpec(memory_space=VMEM if inside else pl.ANY)
            for inside in (False, False, True, True, False, True, True)
        ],
        out_specs=(pl.BlockSpec(memory_space=VMEM),) * 3,
        scratch_shapes=[
            VMEM((half, 2 * rows, enc), BF16),
            VMEM((2 * ny,) + table, jnp.int32),
            VMEM(table, jnp.int32),
            VMEM((8, wanted + -wanted % 128), jnp.int32),
            VMEM((half, wide, enc), BF16),
            VMEM((half, wide, enc), BF16),
            VMEM((wanted, enc), F32),
            VMEM((wanted, enc), BF16),
            VMEM((wanted, enc), BF16),
            VMEM((wanted, width), BF16),
            VMEM((wanted, width), BF16),
            VMEM((8, 128), jnp.int32),
            VMEM((8, 128), jnp.int32),
            VMEM((enc, 2 * width), BF16),
            VMEM((half, wide, enc), BF16),
            VMEM((half, wide, enc), BF16),
            VMEM((half, 2 * rows, enc), BF16),
            VMEM((half, 2 * rows, enc), BF16),
            VMEM((2 * rows, enc), F32),
            VMEM((rows, enc), F32),
            VMEM((nb // X_CORES, 8, 128), F32),
            VMEM((X_CORES, 8, 128), F32),
            VMEM((ny, 8, 128), F32),
            VMEM((nz, 8, 128), F32),
            VMEM((tokens, width), BF16),
            VMEM((tokens, width), BF16),
            VMEM(kv_weight.shape, BF16),
            dma, dma((half, 2, CHUNKS)),
            dma, dma((half + 1, ny - 1)),
            dma, dma,
            dma, dma,
            dma, dma((7, 2)),
            dma, dma((half, 2, CHUNKS)),
            dma, dma((half + 1, ny - 1)),
            dma, dma,
            dma, dma,
            dma, dma,
            dma, dma,
            dma((3,)),
        ],
        compiler_params=pltpu.CompilerParams(
            collective_id=1, has_side_effects=True, vmem_limit_bytes=54 << 20
        ),
    )(
        queries[0], out_grad[0], states.reshape(rows, enc), gain, kv_weight, owners, slots,
    )
    return (
        query_grad[None],
        state_grad.reshape(1, held, length, enc),
        gain_grad,
    )


def solution(mesh):
    ny = Y_SIZE
    nz = mesh.shape["seq"] // ny
    nb = mesh.shape["batch"]
    return jax.shard_map(
        functools.partial(on_device, ny, nz, nb),
        mesh=mesh,
        in_specs=(
            P("batch", "seq", None),
            P("batch", "seq", None),
            P("batch", "seq", None, None),
            P(),
            P("batch", None, None),
            P("batch", "seq", None),
            P("batch", "seq", None),
        ),
        out_specs=(P("batch", "seq", None), P("batch", "seq", None, None), P()),
        check_vma=False,
    )
```

```python
import functools
import math

import jax
import jax.numpy as jnp
from jax import lax
from jax.experimental import pallas as pl
from jax.experimental.pallas import tpu as pltpu
from jax.sharding import PartitionSpec as P

HEAD_DIM = 128
GROUP = 64
EPS = 1e-06
Y_SIZE = 4
CHUNKS = 2
FETCH_ORDER = ((0, 0), (1, 1), (0, 1), (1, 0))
RETURN_ORDER = ((0, 1), (1, 0), (0, 0), (1, 1))
X_CORES = 2
MAIN = 4
CAP = 3

MESH = pl.DeviceIdType.MESH
VMEM = pltpu.VMEM
F32 = jnp.float32
BF16 = jnp.bfloat16


def one_hot(mask):
    return jnp.where(mask, 1.0, 0.0).astype(BF16)


class Place:
    def __init__(self, ny, nz):
        me = lax.axis_index("seq")
        self.ny, self.nz = ny, nz
        self.y = lax.div(me, nz)
        self.z = lax.rem(me, nz)
        self.up = self.at(self.y, lax.rem(self.z + 1, nz))
        self.down = self.at(self.y, lax.rem(self.z + nz - 1, nz))
        order = sorted(range(1, ny), key=lambda j: -min(j, ny - j))
        self.across = [lax.rem(self.y + j, ny) for j in order]

    def at(self, y, z):
        return {"seq": y * self.nz + z}


def remote(src, dst, send_sem, recv_sem, device):
    return pltpu.make_async_remote_copy(
        src_ref=src,
        dst_ref=dst,
        send_sem=send_sem,
        recv_sem=recv_sem,
        device_id=device,
        device_id_type=MESH,
    )


MINOR = (((1,), (1,)), ((), ()))
MAJOR = (((0,), (0,)), ((), ()))


def iota(shape, dim):
    return lax.broadcasted_iota(jnp.int32, shape, dim)


def inverse_norm(values):
    return lax.rsqrt(jnp.mean(values * values, axis=-1, keepdims=True) + EPS)


def kernel(
    ny, nz, nb,
    q_hbm, do_hbm, states_ref, gain_ref, kv_hbm, owners_ref, slots_ref,
    dq_ref, out_ref, gain_out_ref,
    ring, tabs, tab, pos, outs, recv, acc, mine, grad_rows, keys_kept, scores_kept, ids, ids_before, weight,
    back_outs, back, sums_in, sums_out, added, own, by_x, by_core, by_y, by_z, q_ref, do_ref, kv_ref,
    ring_send, ring_recv, y_send, y_recv, tab_send, tab_recv, id_send, id_recv, w_send, w_recv,
    sum_send, sum_recv, back_send, back_recv, x_send, x_recv, core_send, core_recv, gy_send, gy_recv, z_send, z_recv,
    in_sems,
):
    half = nz // 2
    place = Place(ny, nz)
    y, z, b = place.y, place.z, lax.axis_index("batch")
    me = y * nz + z
    rows, width = states_ref.shape
    part = rows // CHUNKS
    wide = outs.shape[1]
    block = wide // ny
    wanted = acc.shape[0]
    pieces = 2 * CAP
    length = block // pieces
    steps_pad = tab.shape[0]
    count = ny * nz
    following = {"seq": lax.rem(me + 1, count)}
    preceding = {"seq": lax.rem(me + count - 1, count)}
    x_peers = [lax.rem(b + j * X_CORES, nb) for j in range(1, nb // X_CORES)]
    z_peers = [lax.rem(z + j, nz) for j in range(1, nz)]
    core = lax.rem(b, X_CORES)
    right = lax.rem(b + X_CORES, nb)
    left = lax.rem(b + nb - X_CORES, nb)
    opposite = lax.rem(b + 2 * X_CORES, nb)
    sibling = b + 1 - 2 * core


    def ring_part(slot, way, chunk):
        return ring.at[slot, pl.ds(way * rows + chunk * part, part)]

    def forward(slot, way, chunk):
        far = isinstance(slot, int) and slot == half - 1
        first = isinstance(slot, int) and slot == 0
        src = ring_part(half - 1, 0, chunk) if first else ring_part(slot - 1, way, chunk)
        dst = ring_part(slot, 1, chunk) if far else ring_part(slot, way, chunk)
        return remote(
            src,
            dst,
            ring_send,
            ring_recv.at[slot, way, chunk],
            place.down if way == 0 else place.up,
        )


    main, rest = MAIN * length, block - MAIN * length

    def exchange(out, into, send, arrived, slot, j):
        there = place.across[j]
        first, size, row = 0, block, slot
        if isinstance(slot, int) and slot == half - 1:
            size = main
        elif isinstance(slot, int) and slot == half:
            first, size, row = ny * main, rest, half - 1
        return remote(
            out.at[row, pl.ds(first + there * size, size)],
            into.at[row, pl.ds(first + y * size, size)],
            send,
            arrived.at[slot, j],
            place.at(there, z),
        )

    def keep(out, into, slot):
        if isinstance(slot, int) and slot == half - 1:
            here = pl.ds(y * main, main)
            into[half - 1, here] = out[half - 1, here]
        elif isinstance(slot, int) and slot == half:
            here = pl.ds(ny * main + y * rest, rest)
            into[half - 1, here] = out[half - 1, here]
        else:
            here = pl.ds(y * block, block)
            into[slot, here] = out[slot, here]

    def across(slot, j):
        return exchange(outs, recv, y_send, y_recv, slot, j)

    def return_across(slot, j):
        return exchange(back_outs, back, back_send, back_recv, slot, j)

    def table_copy(j):
        there = place.across[j]
        return remote(
            tabs.at[ny + there], tabs.at[y], tab_send, tab_recv, place.at(there, z)
        )


    depth = kv_hbm.shape[0]
    cut = (depth + 31) // 32 * 16
    weight_parts = ((0, cut), (cut, depth - cut))

    def weight_copy(channel, number):
        first, size = weight_parts[number]
        if channel == 2:
            shard, device = (left, right) if number == 0 else (right, left)
        else:
            shard = (b, b, None, b, left, right, opposite)[channel]
            device = (right, left, None, sibling, sibling, sibling, sibling)[channel]
        there = weight.at[pl.ds(pl.multiple_of(shard * depth + first, 16), size)]
        return remote(
            there,
            there,
            w_send,
            w_recv.at[channel, number],
            {"batch": device},
        )

    def weights_one():
        answer()
        for number in range(2):
            weight_copy(3, number).start()
        weight_copy(0, 0).wait_recv()
        weight_copy(2, 0).start()
        weight_copy(4, 0).start()
        weight_copy(1, 1).wait_recv()
        weight_copy(2, 1).start()
        weight_copy(5, 1).start()

    def weights_two():
        weight_copy(0, 1).wait_recv()
        weight_copy(4, 1).start()
        weight_copy(1, 0).wait_recv()
        weight_copy(5, 0).start()

    def weights_three():
        for number in range(2):
            weight_copy(2, number).wait_recv()
            weight_copy(6, number).start()


    def part_of(ref, slot, way, chunk):
        return ref.at[slot, pl.ds(way * rows + chunk * part, part)]

    def pass_on(distance, way, chunk):
        far = isinstance(distance, int) and distance == half
        return remote(
            part_of(sums_out, distance - 1, 1 if far else way, chunk),
            part_of(sums_in, distance - 1, way, chunk),
            sum_send,
            sum_recv.at[distance - 1, way, chunk],
            place.up if way == 0 else place.down,
        )

    def all_of(ref, send, arrived):
        return remote(ref, ref, send, arrived, place.up)


    x = lax.div(b, X_CORES)

    def x_copy(j):
        return remote(
            by_x.at[x], by_x.at[x], x_send, x_recv, {"batch": x_peers[j]}
        )

    def core_copy():
        return remote(
            by_core.at[core], by_core.at[core], core_send, core_recv, {"batch": sibling}
        )

    def gy_copy(j):
        return remote(
            by_y.at[y], by_y.at[y], gy_send, gy_recv, place.at(place.across[j], z)
        )

    def z_copy(j):
        return remote(
            by_z.at[z], by_z.at[z], z_send, z_recv, place.at(y, z_peers[j])
        )

    def total(ref):
        result = ref[0]
        for i in range(1, ref.shape[0]):
            result = result + ref[i]
        return result


    kv_in = pltpu.make_async_copy(kv_hbm, kv_ref, in_sems.at[0])
    q_in = pltpu.make_async_copy(q_hbm, q_ref, in_sems.at[1])
    do_in = pltpu.make_async_copy(do_hbm, do_ref, in_sems.at[2])
    for copy in (kv_in, q_in, do_in):
        copy.start()

    gain = gain_ref[...].reshape(1, width)
    values = states_ref[...].astype(F32)
    ring[half - 1, :rows] = (values * inverse_norm(values) * gain).astype(BF16)
    ids[...] = jnp.zeros_like(ids)
    group = owners_ref.shape[2]
    for i in range(owners_ref.shape[1]):
        ids[0:1, i * group : (i + 1) * group] = owners_ref[0, i : i + 1]
        ids[1:2, i * group : (i + 1) * group] = slots_ref[0, i : i + 1]

    barrier = pltpu.get_barrier_semaphore()

    def tell(device):
        pl.semaphore_signal(barrier, inc=1, device_id=device, device_id_type=MESH)

    peers = (
        [place.up, place.down, preceding]
        + [place.at(there, z) for there in place.across]
        + [{"batch": peer} for peer in x_peers]
    )
    for peer in peers:
        tell(peer)

    @pl.when(core == 0)
    def _():
        pl.semaphore_wait(barrier, len(peers))

    @pl.when(core == 1)
    def _():
        pl.semaphore_wait(barrier, len(peers) + 1)

    tell({"batch": sibling})

    def answer():
        @pl.when(core == 0)
        def _():
            pl.semaphore_wait(barrier, 1)

    ids_copy = remote(ids, ids_before, id_send, id_recv, following)
    ids_copy.start()
    for way, chunk in FETCH_ORDER:
        forward(0, way, chunk).start()


    own_count = 2 * group
    request_count = own_count + group
    ids_copy.wait()
    lane = iota(ids.shape, 1)
    merged = jnp.where(lane < own_count, ids[...], pltpu.roll(ids_before[...], group, 1))
    known = (lane < own_count) | ((lane < request_count) & (me > 0))
    owner = jnp.where(known, merged, -1)[0:1]
    slot_id = merged[1:2]
    lane = lane[0:1]
    rank = jnp.where(lane < own_count, 0, CAP - 1)
    wide_owner = jnp.broadcast_to(owner, ids.shape)
    for shift in range(1, 2 * group):
        other = pltpu.roll(wide_owner, shift, 1)[0:1]
        source = lane - shift
        same = (other == owner) & (source >= 0) & (source < group)
        rank = jnp.where(same & (lane >= group) & (lane < own_count), 1, rank)
    column = jnp.zeros_like(owner)
    for j in range(1, ny):
        column = column + jnp.where(owner >= j * nz, 1, 0)
    ahead = owner - column * nz - z
    ahead = jnp.where(ahead < 0, ahead + nz, ahead)
    way = jnp.where(ahead >= half, 1, 0)
    distance = jnp.where(ahead == 0, half, jnp.where(ahead > half, nz - ahead, ahead))
    piece = (1 - way) * CAP + rank
    cell = jnp.where(owner >= 0, column * steps_pad + distance - 1, -1)
    last = jnp.where(
        piece < MAIN, column * MAIN + piece, ny * MAIN + column * (pieces - MAIN) + piece - MAIN
    )
    number = jnp.where(distance == half, last, column * pieces + piece)
    number = jnp.where(owner >= 0, (distance - 1) * ny * pieces + number, -1)
    value = way * rows + slot_id * length + 1

    table_rows, table_lanes = ny * steps_pad, tab.shape[1]
    lanes_of = (table_lanes, lane.shape[1])
    cells = one_hot(iota((table_rows, lane.shape[1]), 0) == cell)

    def found_at(first, size, first_piece):
        row = iota(lanes_of, 0) - (first + y * size)
        inside = (row >= 0) & (row < size)
        return jnp.where(inside, lax.div(row, length) + first_piece, -1)

    def found_by(row_piece):
        chosen = jnp.where(row_piece == piece, value, 0).astype(F32).astype(BF16)
        return lax.dot_general(cells, chosen, MINOR, preferred_element_type=F32)

    whole = found_by(found_at(0, block, 0))
    cut_in_two = found_by(
        jnp.maximum(found_at(0, main, 0), found_at(ny * main, rest, MAIN))
    )
    step_of = lax.rem(iota((table_rows, table_lanes), 0), steps_pad)
    found = jnp.where(step_of == half - 1, cut_in_two, whole).astype(jnp.int32)
    token = lax.rem(iota((table_rows, table_lanes), 1), length)
    table = jnp.where(found > 0, found + token, 0)
    for j in range(ny):
        tabs[ny + j] = table[j * steps_pad : (j + 1) * steps_pad]
    for j in range(ny - 1):
        table_copy(j).start()
    tabs[pl.ds(y, 1)] = tabs[pl.ds(ny + y, 1)]

    spread_of = (pos.shape[1], lane.shape[1])
    spread = one_hot(lax.div(iota(spread_of, 0), length) == iota(spread_of, 1))
    numbers = jnp.broadcast_to(number, ids.shape).astype(F32).astype(BF16)
    placed = lax.dot_general(numbers, spread, MINOR, preferred_element_type=F32).astype(jnp.int32)
    token = lax.rem(iota(placed.shape, 1), length)
    pos[...] = jnp.where(placed >= 0, placed * length + token, -1)

    acc[...] = jnp.zeros_like(acc)
    kv_in.wait()
    own_shard = pl.ds(pl.multiple_of(b * depth, 16), depth)
    weight[own_shard, : kv_ref.shape[2]] = kv_ref[:, 0, :]
    weight[own_shard, kv_ref.shape[2] :] = kv_ref[:, 1, :]
    for number in range(2):
        weight_copy(0, number).start()
        weight_copy(1, 1 - number).start()


    def selected_in(rows_there, first, size):
        row = tab[half - 1 : half, first : first + size]
        return one_hot(iota((rows_there, size), 0) + 1 == row)

    def selected(slot):
        row = tab[pl.ds(slot, 1), :wide]
        return one_hot(iota((2 * rows, wide), 0) + 1 == row)

    def placing(slot):
        return one_hot(iota((wide, wanted), 0) + slot * wide == pos[0:1, :wanted])

    def pick_by(select, shards):
        return lax.dot_general(select, shards, MAJOR, preferred_element_type=F32).astype(BF16)

    def pick(slot):
        if isinstance(slot, int) and slot == half:
            outs[half - 1, ny * main :] = pick_by(
                selected_in(rows, ny * main, ny * rest), ring[half - 1, :rows]
            )
        elif isinstance(slot, int) and slot == half - 1:
            outs[half - 1, : ny * main] = pick_by(
                selected_in(2 * rows, 0, ny * main), ring[half - 1]
            )
        else:
            outs[slot] = pick_by(selected(slot), ring[slot])
        for j in range(ny - 1):
            across(slot, j).start()
        keep(outs, recv, slot)

    def take(slot):
        for j in range(ny - 1):
            across(slot, j).wait_recv()
            if isinstance(slot, int) and slot == half - 1:
                across(half, j).wait_recv()
        acc[...] += lax.dot_general(placing(slot), recv[slot], MAJOR, preferred_element_type=F32)

    def near(slot, last):
        hand_on(slot, last)
        pick(slot)

    def hand_on(slot, last):
        for way, chunk in FETCH_ORDER:
            forward(slot, way, chunk).wait_recv()
            if not last:
                forward(slot + 1, way, chunk).start()
            elif way == chunk:
                forward(half - 1, way, chunk).start()

    services = {2: weights_one, 4: weights_two}
    hand_on(0, half == 2)
    all_of(tabs.at[pl.ds(0, ny - 1)], tab_send, tab_recv).wait()
    asked = tabs[0]
    for j in range(1, ny):
        asked = asked + tabs[j]
    tab[...] = asked
    pick(half)
    pick(0)
    if half > 2:

        @pl.loop(1, half - 2)
        def _(slot):
            near(slot, False)
            take(slot - 1)
            for at, service in services.items():
                if at < half - 2:
                    pl.when(slot == at)(service)

        near(half - 2, True)
        take(half - 3)
    for at, service in services.items():
        if at >= half - 2:
            service()
    weights_three()
    for way in range(2):
        forward(half - 1, way, way).wait_recv()
    pick(half - 1)
    take(half - 2)
    for channel in range(3, 7):
        for number in range(2):
            weight_copy(channel, number).wait_recv()
    take(half - 1)
    mine[...] = acc[...].astype(BF16)


    q_in.wait()
    do_in.wait()
    tokens = q_ref.shape[0]
    scaling = 1.0 / math.sqrt(HEAD_DIM)
    turn = lax.div(iota((wanted, tokens), 1) + 1, GROUP)
    key_group = lax.div(iota((wanted, tokens), 0), GROUP)
    mask = lax.rem(turn + 2, 3) == key_group
    mask = mask & ((turn > 0) | (me > 0))
    pages = mine[...]
    heads_wide = min(8 * HEAD_DIM, q_ref.shape[1])
    steps = q_ref.shape[1] // heads_wide
    acc[...] = jnp.zeros_like(acc)

    @pl.loop(0, steps)
    def _(step):
        here = pl.ds(pl.multiple_of(step * heads_wide, heads_wide), heads_wide)
        there = pl.ds(
            pl.multiple_of((steps + step) * heads_wide, heads_wide), heads_wide
        )
        key_weight, value_weight = weight[:, here], weight[:, there]
        key_all = jnp.dot(pages, key_weight, preferred_element_type=F32).astype(BF16)
        value_all = jnp.dot(pages, value_weight, preferred_element_type=F32).astype(BF16)
        queries, grads = q_ref[:, here], do_ref[:, here]
        key_grads, value_grads = [], []
        keys_kept[:, here] = key_all
        for head in range(heads_wide // HEAD_DIM):
            columns = slice(head * HEAD_DIM, (head + 1) * HEAD_DIM)
            query, grad = queries[:, columns], grads[:, columns]
            key, val = key_all[:, columns], value_all[:, columns]
            scores = lax.dot_general(key, query, MINOR, preferred_element_type=F32) * scaling
            weights = jnp.where(mask, jnp.exp(scores), 0.0)
            over = jnp.sum(weights, axis=0, keepdims=True)
            probability = weights * (1.0 / jnp.where(over == 0.0, 1.0, over))
            grad_probability = lax.dot_general(val, grad, MINOR, preferred_element_type=F32)
            delta = jnp.sum(probability * grad_probability, axis=0, keepdims=True)
            grad_scores = (probability * (grad_probability - delta) * scaling).astype(BF16)
            low = probability.astype(BF16)
            scores_kept[:, pl.ds(here.start + head * HEAD_DIM, HEAD_DIM)] = grad_scores
            key_grads.append(jnp.dot(grad_scores, query, preferred_element_type=F32))
            value_grads.append(jnp.dot(low, grad, preferred_element_type=F32))
        key_grad = jnp.concatenate(key_grads, axis=1).astype(BF16)
        value_grad = jnp.concatenate(value_grads, axis=1).astype(BF16)
        change = lax.dot_general(key_grad, key_weight, MINOR, preferred_element_type=F32)
        change += lax.dot_general(value_grad, value_weight, MINOR, preferred_element_type=F32)
        acc[...] += change

    grad_rows[...] = acc[...].astype(BF16)

    def query_grad(head):
        here = pl.ds(pl.multiple_of(head * HEAD_DIM, HEAD_DIM), HEAD_DIM)
        dq_ref[:, here] = lax.dot_general(
            scores_kept[:, here], keys_kept[:, here], MAJOR, preferred_element_type=F32
        ).astype(BF16)


    def scatter(slot):
        back_outs[slot] = jnp.dot(placing(slot), grad_rows[...], preferred_element_type=F32).astype(BF16)
        for j in range(ny - 1):
            return_across(slot, j).start()
        keep(back_outs, back, slot)

    def scatter_rest():
        for j in range(ny - 1):
            return_across(half, j).start()
        keep(back_outs, back, half)

    def gather_by(select, blocks):
        return jnp.dot(select, blocks, preferred_element_type=F32)

    def gather(slot):
        for j in range(ny - 1):
            return_across(slot, j).wait_recv()
        added[...] = gather_by(selected(slot), back[slot])

    def gather_far():
        for j in range(ny - 1):
            return_across(half - 1, j).wait_recv()
        added[...] = gather_by(
            selected_in(2 * rows, 0, ny * main), back[half - 1, : ny * main]
        )

    def gather_rest():
        for j in range(ny - 1):
            return_across(half, j).wait_recv()
        own[...] += gather_by(
            selected_in(rows, ny * main, ny * rest), back[half - 1, ny * main :]
        )

    def relay(distance, first):
        gather(distance - 1)
        for way, chunk in RETURN_ORDER:
            here = pl.ds(way * rows + chunk * part, part)
            total_here = added[here]
            if not first or way == chunk:
                pass_on(distance + 1, way, chunk).wait_recv()
                total_here = total_here + sums_in[distance, here].astype(F32)
            sums_out[distance - 1, here] = total_here.astype(BF16)
            pass_on(distance, way, chunk).start()

    def pass_sent(ref, send):
        every = ref.at[pl.ds(0, half - 1)]
        all_of(every, send, send).wait_send()
        last = ref.at[half - 1, pl.ds(0, rows)]
        all_of(last, send, send).wait_send()

    def across_sent(ref, send):
        every = ref.at[:, pl.ds(0, wide - block)]
        all_of(every, send, send).wait_send()

    def fetch_sent():
        pass_sent(ring, ring_send)
        across_sent(outs, y_send)
        all_of(weight.at[pl.ds(0, 7 * depth)], w_send, w_send).wait_send()

    def gain_one():
        lanes = width // 128
        products = jnp.sum(grad_rows[...].astype(F32) * mine[...].astype(F32), axis=0, keepdims=True)
        products = products / gain
        by_x[pl.ds(x, 1)] = jnp.zeros_like(by_x[pl.ds(x, 1)])
        for i in range(lanes):
            by_x[x, i : i + 1] = products[:, i * 128 : (i + 1) * 128]
        for j in range(len(x_peers)):
            x_copy(j).start()

    def gain_two():
        all_of(by_x.at[pl.ds(0, len(x_peers))], x_send, x_recv).wait()
        by_core[core] = total(by_x)
        core_copy().start()

    def gain_three():
        core_copy().wait()
        by_y[y] = total(by_core)
        for j in range(ny - 1):
            gy_copy(j).start()

    def gain_four():
        all_of(by_y.at[pl.ds(0, ny - 1)], gy_send, gy_recv).wait()
        by_z[z] = total(by_y)
        for j in range(nz - 1):
            z_copy(j).start()

    scatter(half - 1)
    scatter(half - 2)
    gain_one()
    fetch_sent()
    if half > 2:
        scatter(half - 3)
    gather_far()
    sums_out[half - 1, pl.ds(rows, rows)] = added[pl.ds(rows, rows)].astype(BF16)
    for way in range(2):
        pass_on(half, way, way).start()
    own[...] = added[:rows]
    relay(half - 1, True)
    scatter_rest()
    gain_two()
    heads = q_ref.shape[1] // HEAD_DIM
    turns = max(half - 3, 0)
    each = heads // turns if turns else 0
    for head in range(each * turns, heads):
        query_grad(head)
    if half > 2:

        @pl.loop(0, half - 3)
        def _(i):
            distance = half - 2 - i
            scatter(distance - 2)
            relay(distance, False)
            pl.when(i == max(0, half - 6))(gain_three)
            for head in range(each):
                query_grad(i * each + head)

    else:
        gain_three()
    gain_four()
    gather_rest()
    if half > 2:
        relay(1, False)

    all_of(by_z.at[pl.ds(0, nz - 1)], z_send, z_recv).wait()
    result = total(by_z)
    for i in range(width // 128):
        gain_out_ref[i * 128 : (i + 1) * 128] = result[i]

    for chunk in range(CHUNKS):
        here = pl.ds(chunk * part, part)
        for way in range(2):
            pass_on(1, way, chunk).wait_recv()
        normed_grad = own[here] + sums_in[0, here].astype(F32)
        normed_grad = normed_grad + sums_in[0, pl.ds(rows + chunk * part, part)].astype(F32)
        values = states_ref[here].astype(F32)
        inverse = inverse_norm(values)
        scaled = normed_grad * gain
        inner = jnp.mean(scaled * values, axis=-1, keepdims=True)
        out_ref[here] = (
            inverse * scaled - values * (inverse * inverse * inverse * inner)
        ).astype(BF16)

    pass_sent(sums_out, sum_send)
    across_sent(back_outs, back_send)


def on_device(ny, nz, nb, queries, out_grad, states, gain, kv_weight, owners, slots):
    held, length, enc = states.shape[1:]
    tokens, width = queries.shape[1:]
    half, rows = nz // 2, held * length
    wanted = owners.shape[1] * owners.shape[2] * 3 // 2 * length
    wide = ny * 2 * CAP * length
    table = (max(8, half), wide + -wide % 128)
    dma = pltpu.SemaphoreType.DMA
    query_grad, state_grad, gain_grad = pl.pallas_call(
        functools.partial(kernel, ny, nz, nb),
        out_shape=(
            jax.ShapeDtypeStruct((tokens, width), BF16),
            jax.ShapeDtypeStruct((rows, enc), BF16),
            jax.ShapeDtypeStruct((enc,), F32),
        ),
        in_specs=[
            pl.BlockSpec(memory_space=VMEM if inside else pl.ANY)
            for inside in (False, False, True, True, False, True, True)
        ],
        out_specs=(pl.BlockSpec(memory_space=VMEM),) * 3,
        scratch_shapes=[
            VMEM((half, 2 * rows, enc), BF16),
            VMEM((2 * ny,) + table, jnp.int32),
            VMEM(table, jnp.int32),
            VMEM((8, wanted + -wanted % 128), jnp.int32),
            VMEM((half, wide, enc), BF16),
            VMEM((half, wide, enc), BF16),
            VMEM((wanted, enc), F32),
            VMEM((wanted, enc), BF16),
            VMEM((wanted, enc), BF16),
            VMEM((wanted, width), BF16),
            VMEM((wanted, width), BF16),
            VMEM((8, 128), jnp.int32),
            VMEM((8, 128), jnp.int32),
            VMEM((enc, 2 * width), BF16),
            VMEM((half, wide, enc), BF16),
            VMEM((half, wide, enc), BF16),
            VMEM((half, 2 * rows, enc), BF16),
            VMEM((half, 2 * rows, enc), BF16),
            VMEM((2 * rows, enc), F32),
            VMEM((rows, enc), F32),
            VMEM((nb // X_CORES, 8, 128), F32),
            VMEM((X_CORES, 8, 128), F32),
            VMEM((ny, 8, 128), F32),
            VMEM((nz, 8, 128), F32),
            VMEM((tokens, width), BF16),
            VMEM((tokens, width), BF16),
            VMEM(kv_weight.shape, BF16),
            dma, dma((half, 2, CHUNKS)),
            dma, dma((half + 1, ny - 1)),
            dma, dma,
            dma, dma,
            dma, dma((7, 2)),
            dma, dma((half, 2, CHUNKS)),
            dma, dma((half + 1, ny - 1)),
            dma, dma,
            dma, dma,
            dma, dma,
            dma, dma,
            dma((3,)),
        ],
        compiler_params=pltpu.CompilerParams(
            collective_id=1, has_side_effects=True, vmem_limit_bytes=54 << 20
        ),
    )(
        queries[0], out_grad[0], states.reshape(rows, enc), gain, kv_weight, owners, slots,
    )
    return (
        query_grad[None],
        state_grad.reshape(1, held, length, enc),
        gain_grad,
    )


def solution(mesh):
    ny = Y_SIZE
    nz = mesh.shape["seq"] // ny
    nb = mesh.shape["batch"]
    return jax.shard_map(
        functools.partial(on_device, ny, nz, nb),
        mesh=mesh,
        in_specs=(
            P("batch", "seq", None),
            P("batch", "seq", None),
            P("batch", "seq", None, None),
            P(),
            P("batch", None, None),
            P("batch", "seq", None),
            P("batch", "seq", None),
        ),
        out_specs=(P("batch", "seq", None), P("batch", "seq", None, None), P()),
        check_vma=False,
    )
```
